256 devices in a mesh: ka: 64 (over z, x_hi, y), row: 4 (over x_lo, core).
Axes of the slice: x: 4 (x_hi: 2, x_lo: 2; x = x_hi * 2 + x_lo), y: 4, z: 8, core: 2. Of those that a mesh axis runs over, the one named last changes fastest.
Arguments:
- occupied: bfloat16 [64, 8, 16384], P('ka', None, 'row'), may hold values from -6 to 6
- empty: bfloat16 [64, 64, 16384], P('ka', None, 'row'), may hold values from -6 to 6
- occ_energy: bfloat16 [64, 8], P('ka'), may hold values from -3 to -0.5
- emp_energy: bfloat16 [64, 64], P('ka'), may hold values from 0.5 to 3
- partner: int32 [2, 64], replicated, may hold values from 0 to 63, as said below
- gvecs: int32 [2, 384, 3], replicated, may hold values from -4 to 4
Outputs:
- polarity: float32 [2, 768, 768], P(None, 'ka', 'row')
The draws below stay inside these ranges and needn't reach their ends.
Inputs may be any that keep to these rules, and one draw needn't show every extreme that they name: partner[q, k] is the index of k + q_q on the periodic 4 x 4 x 4 grid of k-points, k = (i * 4 + j) * 4 + l, where each momentum q_q is a nonzero step along the first dimension only.
All inputs are finite; a program needn't handle non-finite values.
Results may differ from the reference program's by a relative error of at most 0.004.
Values may be sent and summed in bfloat16 or wider, within the bound.
A program may use at most 64 MiB of HBM per device.

```python
import math
import jax
import jax.numpy as jnp
from jax import lax

NO = 8
NE = 64
NG = 384
Q = 2
GY = 16
GZ = 32
R = 16384
GX = 32
NK = 64
KX = 4
KY = 4
KZ = 4


def draw_partner(key, part):
    points = jnp.arange(NK, dtype=jnp.int32)
    point_x = points // (KY * KZ)
    rest = points % (KY * KZ)
    tables = []
    for moment in range(Q):
        subkey = jax.random.fold_in(key, 101 + moment)
        move_x = jax.random.randint(subkey, (), 1, KX).astype(jnp.int32)
        tables.append((point_x + move_x) % KX * (KY * KZ) + rest)
    return jnp.stack(tables).astype(jnp.int32)


def place_ends(values, key, least, largest):
    dims = values.shape
    place = [jax.random.randint(jax.random.fold_in(key, axis), (), 0, dims[axis]) for axis in range(len(dims))]
    values = values.at[tuple(place)].set(least)
    longest = dims.index(max(dims))
    place[longest] = (place[longest] + 1) % dims[longest]
    return values.at[tuple(place)].set(largest)


def shard_levels(rng, extent, shards, smallest, largest):
    def one(position, parts):
        heights = jax.random.uniform(jax.random.fold_in(jax.random.fold_in(rng, 6), position), (parts,), jnp.float32, smallest / len(shards), largest / len(shards))
        return jnp.repeat(jnp.exp(heights), extent[position] // parts).reshape((-1,) + (1,) * (len(extent) - position - 1))

    loudness = one(*shards[0])
    for cut in shards[1:]:
        loudness = loudness * one(*cut)
    return loudness


def scatter_about(stream_key, dims, width, reach, shards=(), held_as=jnp.bfloat16):
    factor_of = shard_levels(stream_key, dims, shards, -0.22, 0.18) if shards else 1.0
    entries = jax.random.normal(stream_key, dims, jnp.float32) * width * factor_of
    return jnp.minimum(jnp.maximum(entries, -reach), reach).astype(held_as)


def setup_inputs(seed: int = 0) -> dict:
    key_list = jax.random.split(jax.random.key(seed), 7)
    occupied = scatter_about(key_list[0], (NK, NO, R), 1.0, 6.0, ((0, 64), (2, 4)))
    empty = scatter_about(key_list[1], (NK, NE, R), 1.0, 6.0, ((0, 64), (2, 4)))
    occ_energy = jnp.clip(-3.0 + 2.5 * jax.random.uniform(key_list[2], (NK, NO), jnp.float32) ** shard_levels(key_list[2], (NK, NO), ((0, 64),), -0.2, 0.2), -3.0, -0.5).astype(jnp.bfloat16)
    emp_energy = jnp.clip(0.5 + 2.5 * jax.random.uniform(key_list[3], (NK, NE), jnp.float32) ** shard_levels(key_list[3], (NK, NE), ((0, 64),), -0.2, 0.2), 0.5, 3.0).astype(jnp.bfloat16)
    partner = draw_partner(jax.random.fold_in(key_list[6], 71), 0)
    gvecs = place_ends(jax.random.randint(key_list[5], (Q, NG, 3), -4, 5), jax.random.fold_in(key_list[5], 1), -4, 4).astype(jnp.int32)
    return dict(occupied=occupied, empty=empty, occ_energy=occ_energy, emp_energy=emp_energy, partner=partner, gvecs=gvecs)


def phase_table(plane_waves, start_point, point_count, grid_x, grid_y, grid_z):
    grid_total = grid_x * grid_y * grid_z
    points = start_point + lax.iota(jnp.int32, point_count)
    coord_z = points % grid_z
    coord_y = (points // grid_z) % grid_y
    coord_x = points // (grid_y * grid_z)
    phase_index = (plane_waves[:, 0:1] * coord_x[None, :] * (grid_y * grid_z)
                   + plane_waves[:, 1:2] * coord_y[None, :] * (grid_x * grid_z)
                   + plane_waves[:, 2:3] * coord_z[None, :] * (grid_x * grid_y)) % grid_total
    angle = phase_index.astype(jnp.float32) * (2.0 * math.pi / grid_total)
    return jnp.concatenate([jnp.cos(angle), jnp.sin(angle)], axis=0).astype(jnp.bfloat16)


def reference(occupied, empty, occ_energy, emp_energy, partner, gvecs):
    outputs = []
    for moment in range(Q):
        table_q = phase_table(gvecs[moment], 0, R, GX, GY, GZ)

        def accumulate(index, carry):
            source = partner[moment, index].astype(jnp.int32)
            occ_block = lax.dynamic_index_in_dim(occupied, index, 0, keepdims=False)
            emp_block = lax.dynamic_index_in_dim(empty, source, 0, keepdims=False)
            occ_level = lax.dynamic_index_in_dim(occ_energy, index, 0, keepdims=False)
            emp_level = lax.dynamic_index_in_dim(emp_energy, source, 0, keepdims=False)
            density = (occ_block.astype(jnp.float32)[:, None, :] * emp_block.astype(jnp.float32)[None, :, :]).reshape(NO * NE, R).astype(jnp.bfloat16)
            projected = lax.dot_general(density, table_q, (((1,), (1,)), ((), ())), preferred_element_type=jnp.float32) * (1.0 / R)
            weight = (1.0 / (emp_level.astype(jnp.float32)[None, :] - occ_level.astype(jnp.float32)[:, None])).reshape(NO * NE)
            left_side = projected.astype(jnp.bfloat16)
            right_side = (weight[:, None] * projected).astype(jnp.bfloat16)
            return carry + lax.dot_general(left_side, right_side, (((0,), (0,)), ((), ())), preferred_element_type=jnp.float32)

        outputs.append(lax.fori_loop(0, NK, accumulate, jnp.zeros((2 * NG, 2 * NG), jnp.float32)))
    return jnp.stack(outputs)
```

```python
import math

import jax
import jax.numpy as jnp
import numpy as np
from jax import lax
from jax.experimental import pallas as pl
from jax.experimental.pallas import tpu as pltpu
from jax.sharding import PartitionSpec as P

MESH = pl.DeviceIdType.MESH
F32 = jnp.float32
BF16 = jnp.bfloat16
NO = 8
NB = 32
NG = 384
PTS = 4096
YZ = 512
GY = 16
GZ = 32
NX = 8
COLS = 2 * NG


def yz_table():
    point = np.arange(YZ)
    y, z = point // GZ, point % GZ
    table = np.zeros((YZ, 128), np.float64)
    for g1 in range(-4, 5):
        for g2 in range(5):
            turn = 2 * math.pi * ((g1 * y * 2 + g2 * z) % 32) / 32
            column = (g1 + 4) * 5 + g2
            table[:, column] = np.cos(turn)
            table[:, 64 + column] = np.sin(turn)
    return table.astype(np.float32)


def row_order():
    a = np.arange(COLS)
    z, xh, y, i = a // 96, a // 48 % 2, a // 12 % 4, a % 12
    first = xh * 192 + y * 48 + (z % 4) * 12 + i
    second = 384 + y * 96 + xh * 48 + (z % 4) * 12 + i
    return np.where(z < 4, first, second).astype(np.int32)


def kernel(
    occ_ref, emp_ref, oe_ref, ee_ref, partner_ref, wave_ref, yz_ref, out_ref,
    shift, oe_src, oe_shift, efull, osel, ofull, wtab, utab, vtab, ybuf, proj, gram,
    ra1, rb1, sa2, sb2, ra2, rb2, sa3, sb3, st3, r3,
    zsend, zrecv, gsend, grecv, rsend, rrecv, fsend, frecv, lsem,
):
    ka, row = lax.axis_index("ka"), lax.axis_index("row")
    z, xh, y = ka // 8, ka // 4 % 2, ka % 4
    xl, core = row // 2, row % 2
    x = xh * 2 + xl

    def device(z_, x_, y_, core_):
        return (z_ * 8 + (x_ // 2) * 4 + y_, (x_ % 2) * 2 + core_)

    sibling = (ka, xl * 2 + 1 - core)
    across = (ka, (1 - xl) * 2 + core)
    diagonal = (ka, (1 - xl) * 2 + 1 - core)
    x_peer = [device(z, (x + d) % 4, y, core) for d in range(1, 4)]
    y_peer = [device(z, x, (y + d) % 4, core) for d in range(1, 4)]
    z_peer = [[device((z + d) % 8, x, y, core if r == 0 else 1 - core) for r in range(2)] for d in range(8)]

    barrier = pltpu.get_barrier_semaphore()
    peers = [sibling, across, diagonal] + x_peer + y_peer + [z_peer[d][r] for d in range(1, 8) for r in range(2)]
    for peer in peers:
        pl.semaphore_signal(barrier, inc=1, device_id=peer, device_id_type=MESH)

    eye = lax.broadcasted_iota(jnp.int32, (NO, NO), 0) == lax.broadcasted_iota(jnp.int32, (NO, NO), 1)
    levels = jnp.broadcast_to(oe_ref[...].astype(F32), (NO, NO))
    column = jnp.sum(jnp.where(eye, levels, 0.0), axis=1, keepdims=True)
    oe_src[...] = jnp.broadcast_to(column, (NO, 128))
    pl.semaphore_wait(barrier, len(peers))

    def send(src, dst, sends, recvs, index, peer):
        copy = pltpu.make_async_remote_copy(
            src_ref=src, dst_ref=dst, send_sem=sends.at[index], recv_sem=recvs.at[index],
            device_id=peer, device_id_type=MESH,
        )
        copy.start()
        return copy

    shifts = []
    for s in range(1, 4):
        shifts.append(send(occ_ref.at[0], shift.at[s - 1], zsend, zrecv, s - 1, z_peer[2 * s][0]))
        shifts.append(send(oe_src, oe_shift.at[s - 1], zsend, zrecv, s + 2, z_peer[2 * s][0]))
    theirs = []
    for part in range(2):
        bands = pl.ds(pl.multiple_of((1 - xl) * NB + part * 16, 16), 16)
        theirs.append(send(emp_ref.at[0, bands], efull.at[2, pl.ds(part * 16, 16)], gsend, grecv, part, across))
    own_bands = pl.ds(pl.multiple_of(xl * NB, NB), NB)
    beside = send(emp_ref.at[0, own_bands], efull.at[1], gsend, grecv, 2, sibling)
    local = pltpu.make_async_copy(emp_ref.at[0, own_bands], efull.at[0], lsem)
    local.start()

    wave = wave_ref[core]
    g0, g1, g2, order = wave[0:1], wave[1:2], wave[2:3], wave[3:4]
    flip = jnp.where(g2 < 0, -1, 1)
    group = (flip * g1 + 4) * 5 + flip * g2
    slot_x = lax.broadcasted_iota(jnp.int32, (4 * NX, COLS), 0)
    other_core, other_xl = (slot_x // NX) % 2, slot_x // (2 * NX)
    src_core = core + other_core - 2 * core * other_core
    src_xl = xl + other_xl - 2 * xl * other_xl
    plane = (src_xl * 2 + src_core) * NX + slot_x % NX
    quarter = jnp.where(lax.broadcasted_iota(jnp.int32, (4 * NX, COLS), 1) < NG, 0, 8)
    turn = ((g0 * plane - quarter) & 31).astype(F32) * (2.0 * math.pi / 32)
    utab[...] = jnp.cos(turn)
    vtab[...] = jnp.sin(turn) * (-flip).astype(F32)
    chosen = lax.broadcasted_iota(jnp.int32, (64, COLS), 0) == group

    for slot in range(4):
        def fill(i, carry):
            u = utab[pl.ds(slot * NX + i, 1), :]
            v = vtab[pl.ds(slot * NX + i, 1), :]
            base = pl.multiple_of(i * 128, 128)
            wtab[slot, pl.ds(base, 64), :] = jnp.where(chosen, u, 0.0).astype(BF16)
            wtab[slot, pl.ds(base + 64, 64), :] = jnp.where(chosen, v, 0.0).astype(BF16)
            return carry

        lax.fori_loop(0, NX, fill, 0)

    theirs[0].wait_recv()
    passed = [send(efull.at[2, pl.ds(0, 16)], efull.at[3, pl.ds(0, 16)], gsend, grecv, 3, sibling)]
    for copy in shifts:
        copy.wait_recv()
    steps = [jnp.clip(partner_ref[q, 0] // 16, 1, 3) - 1 for q in range(2)]
    for q in range(2):
        osel[q] = shift[steps[q]]
    gathers = [
        send(osel.at[core], ofull.at[2], gsend, grecv, 6, across),
        send(osel.at[1 - core], ofull.at[3], gsend, grecv, 7, diagonal),
        send(osel.at[1 - core], ofull.at[1], gsend, grecv, 5, sibling),
    ]
    ofull[0] = osel[core]
    theirs[1].wait_recv()
    passed.append(send(efull.at[2, pl.ds(16, 16)], efull.at[3, pl.ds(16, 16)], gsend, grecv, 4, sibling))

    oe = jnp.where(core == 0, oe_shift[steps[0]], oe_shift[steps[1]])
    pick = lax.broadcasted_iota(jnp.int32, (NB, 2 * NB), 1) == lax.broadcasted_iota(jnp.int32, (NB, 2 * NB), 0) + xl * NB
    ee = jnp.broadcast_to(ee_ref[...].astype(F32), (NB, 2 * NB))
    ee = jnp.sum(jnp.where(pick, ee, 0.0), axis=1, keepdims=True)
    weight = jnp.concatenate([1.0 / (ee - oe[v : v + 1, 0:1]) for v in range(NO)], axis=0)

    for slot in range(4):
        if slot == 0:
            local.wait()
        elif slot == 1:
            beside.wait_recv()
            gathers[2].wait_recv()
        elif slot == 2:
            gathers[0].wait_recv()
        else:
            gathers[1].wait_recv()
            passed[0].wait_recv()
            passed[1].wait_recv()

        def project(i, carry):
            lanes = pl.ds(pl.multiple_of(i * YZ, YZ), YZ)
            e = efull[slot, :, lanes].astype(F32)
            o = ofull[slot, :, lanes].astype(F32)
            density = jnp.concatenate([(o[v : v + 1] * e).astype(BF16) for v in range(NO)], axis=0)
            part = jnp.dot(density, yz_ref[...], preferred_element_type=F32)
            ybuf[:, pl.ds(pl.multiple_of(i * 128, 128), 128)] = part.astype(BF16)
            return carry

        lax.fori_loop(0, NX, project, 0)
        term = jnp.dot(ybuf[...], wtab[slot], preferred_element_type=F32)
        proj[...] = term if slot == 0 else proj[...] + term

    value = proj[...] * (1.0 / (4 * PTS))
    left = value.astype(BF16)
    right = (weight * value).astype(BF16)
    ordering = jnp.where(lax.broadcasted_iota(jnp.int32, (COLS, COLS), 0) == order, 1.0, 0.0).astype(BF16)
    left_t = lax.dot_general(ordering, left, (((1,), (1,)), ((), ())), preferred_element_type=F32).astype(BF16)
    gram[...] = jnp.dot(left_t, right, preferred_element_type=F32).astype(BF16)

    def a_block(x_):
        return pl.ds(pl.multiple_of(x_ // 2 * 192, 192), 192), pl.ds(pl.multiple_of(x_ % 2 * 384, 384), 384)

    def b_block(y_):
        return pl.ds(pl.multiple_of(384 + y_ * 96, 96), 96)

    first_a, first_b = [], []
    for d in (2, 1, 3):
        rows, cols = a_block((x + d) % 4)
        first_a.append(send(gram.at[rows, cols], ra1.at[d - 1], rsend, rrecv, d - 1, x_peer[d - 1]))
        first_b.append(send(gram.at[b_block((y + d) % 4)], rb1.at[d - 1], rsend, rrecv, d + 2, y_peer[d - 1]))
    for copy in first_a:
        copy.wait_recv()
    rows, cols = a_block(x)
    total = gram[rows, cols].astype(F32)
    for d in range(3):
        total = total + ra1[d].astype(F32)
    sa2[...] = total.astype(BF16)
    second = []
    for d in (2, 1, 3):
        part = pl.ds(pl.multiple_of((y + d) % 4 * 48, 48), 48)
        second.append(send(sa2.at[part], ra2.at[d - 1], rsend, rrecv, d + 5, y_peer[d - 1]))
    for copy in first_b:
        copy.wait_recv()
    total = gram[b_block(y), :].astype(F32)
    for d in range(3):
        total = total + rb1[d].astype(F32)
    sb2[...] = total.astype(BF16)
    for d in (2, 1, 3):
        to = (x + d) % 4
        part = pl.ds(pl.multiple_of(to // 2 * 48, 48), 48)
        cols = pl.ds(pl.multiple_of(to % 2 * 384, 384), 384)
        second.append(send(sb2.at[part, cols], rb2.at[d - 1], rsend, rrecv, d + 8, x_peer[d - 1]))
    for copy in second:
        copy.wait_recv()
    total = sa2[pl.ds(pl.multiple_of(y * 48, 48), 48), :].astype(F32)
    for d in range(3):
        total = total + ra2[d].astype(F32)
    sa3[0, 0:48] = total
    sa3[1, 0:48] = pltpu.roll(total, 192, 1)
    total = sb2[pl.ds(pl.multiple_of(xh * 48, 48), 48), pl.ds(pl.multiple_of(xl * 384, 384), 384)].astype(F32)
    for d in range(3):
        total = total + rb2[d].astype(F32)
    sb3[0, 0:48] = total
    sb3[1, 0:48] = pltpu.roll(total, 192, 1)

    for to in range(8):
        source = sa3 if to < 4 else sb3
        for half in range(2):
            st3[to, half] = source[half, pl.ds(to % 4 * 12, 16), 0:256].astype(BF16)
    third = []
    for d in (4, 3, 5, 2, 6, 1, 7, 0):
        for r in range(2):
            if d or r:
                to = (z + d) % 8
                half = core if r == 0 else 1 - core
                third.append(send(st3.at[to, half], r3.at[d, r], fsend, frecv, d * 2 + r, z_peer[d][r]))
    for copy in third:
        copy.wait_recv()
    total = st3[z, core].astype(F32)
    for d in range(1, 8):
        total = total + r3[d, 0].astype(F32)
    out_ref[core] = total[0:12, 0:192]
    total = r3[0, 1].astype(F32)
    for d in range(1, 8):
        total = total + r3[d, 1].astype(F32)
    out_ref[1 - core] = total[0:12, 0:192]

    for copy in shifts + theirs + [beside] + passed + gathers + first_a + first_b + second + third:
        copy.wait_send()


def per_device(occupied, empty, occ_energy, emp_energy, partner, gvecs):
    waves = jnp.swapaxes(gvecs, 1, 2)
    waves = jnp.concatenate([waves, waves], axis=2)
    order = jnp.broadcast_to(jnp.asarray(row_order()), (2, 1, COLS))
    waves = jnp.concatenate([waves, order, jnp.zeros((2, 4, COLS), jnp.int32)], axis=1)
    vmem = pl.BlockSpec(memory_space=pltpu.VMEM)
    hbm = pl.BlockSpec(memory_space=pl.ANY)
    smem = pl.BlockSpec(memory_space=pltpu.SMEM)
    dma = pltpu.SemaphoreType.DMA
    return pl.pallas_call(
        kernel,
        out_shape=jax.ShapeDtypeStruct((2, 12, 192), F32),
        in_specs=[hbm, hbm, vmem, vmem, smem, vmem, vmem],
        out_specs=vmem,
        scratch_shapes=[
            pltpu.VMEM((3, NO, PTS), BF16),
            pltpu.VMEM((NO, 128), F32),
            pltpu.VMEM((3, NO, 128), F32),
            pltpu.VMEM((4, NB, PTS), BF16),
            pltpu.VMEM((2, NO, PTS), BF16),
            pltpu.VMEM((4, NO, PTS), BF16),
            pltpu.VMEM((4, NX * 128, COLS), BF16),
            pltpu.VMEM((4 * NX, COLS), F32),
            pltpu.VMEM((4 * NX, COLS), F32),
            pltpu.VMEM((NO * NB, NX * 128), BF16),
            pltpu.VMEM((NO * NB, COLS), F32),
            pltpu.VMEM((COLS, COLS), BF16),
            pltpu.VMEM((3, 192, 384), BF16),
            pltpu.VMEM((3, 96, COLS), BF16),
            pltpu.VMEM((192, 384), BF16),
            pltpu.VMEM((96, COLS), BF16),
            pltpu.VMEM((3, 48, 384), BF16),
            pltpu.VMEM((3, 48, 384), BF16),
            pltpu.VMEM((2, 64, 384), F32),
            pltpu.VMEM((2, 64, 384), F32),
            pltpu.VMEM((8, 2, 16, 256), BF16),
            pltpu.VMEM((8, 2, 16, 256), BF16),
            dma((6,)), dma((6,)), dma((8,)), dma((8,)), dma((12,)), dma((12,)), dma((16,)), dma((16,)), dma,
        ],
        compiler_params=pltpu.CompilerParams(
            collective_id=0, has_side_effects=True, vmem_limit_bytes=48 * 1024 * 1024
        ),
    )(occupied, empty, occ_energy, emp_energy, partner, waves, jnp.asarray(yz_table()).astype(BF16))


def solution(mesh):
    placed = (P("ka", None, "row"), P("ka", None, "row"), P("ka", None), P("ka", None), P(), P())
    return jax.shard_map(
        per_device, mesh=mesh, in_specs=placed, out_specs=P(None, "ka", "row"), check_vma=False
    )
```

```python
import math

import jax
import jax.numpy as jnp
import numpy as np
from jax import lax
from jax.experimental import pallas as pl
from jax.experimental.pallas import tpu as pltpu
from jax.sharding import PartitionSpec as P

MESH = pl.DeviceIdType.MESH
F32 = jnp.float32
BF16 = jnp.bfloat16
NO = 8
NB = 32
NG = 384
PTS = 4096
HALF = PTS // 2
YZ = 512
GZ = 32
COLS = 2 * NG
PAIRS = NO * NB
WIDE = (256, 128)
START = (0, 512)
BLOCKS = (0, 1, 3, 4, 6, 7, 9, 10, 2, 5, 8, 11)
PIECES = ((0, 0), (0, 1), (1, 0), (1, 1), (2, 0), (3, 0), (2, 1), (3, 1))
DIST = (2, 1, 3)


def yz_table():
    point = np.arange(YZ)
    y, z = point // GZ, point % GZ
    table = np.zeros((YZ, 128), np.float64)
    for g1 in range(-4, 5):
        for g2 in range(5):
            turn = 2 * math.pi * ((g1 * y * 2 + g2 * z) % 32) / 32
            column = (g1 + 4) * 5 + g2
            table[:, column] = np.cos(turn)
            table[:, 64 + column] = np.sin(turn)
    return table.astype(np.float32)


def row_order():
    a = np.concatenate([np.arange(64) + 64 * block for block in BLOCKS])
    z, xh, y, i = a // 96, a // 48 % 2, a // 12 % 4, a % 12
    first = xh * 192 + y * 48 + (z % 4) * 12 + i
    second = 384 + y * 96 + xh * 48 + (z % 4) * 12 + i
    return np.where(z < 4, first, second).astype(np.int32).reshape(1, COLS)


def kernel(
    occ_hbm, emp_hbm, oe_ref, ee_ref, partner_ref, wave_ref, order_ref, yz_hbm, out_ref,
    shift0, shift1, oe_src, oe_shift, efull, osel, ofull, yz, wtab, utab, vtab, ybuf, proj, ordering, left_t, right,
    ga0, ga1, gb0, gb1, ra0, ra1, rb0, rb1, ta0, ta1, tb0, tb1, sa0, sa1, sb0, sb1,
    qa0, qa1, qb0, qb1, fa0, fa1, fb0, fb1, st0, st1, r30, r31,
    zsend, zrecv, gsend, grecv, rsend, rrecv, fsend, frecv, lsem,
):
    shift = (shift0, shift1)
    ga, gb, ra, rb = (ga0, ga1), (gb0, gb1), (ra0, ra1), (rb0, rb1)
    ta, tb, sa, sb = (ta0, ta1), (tb0, tb1), (sa0, sa1), (sb0, sb1)
    qa, qb, fa, fb = (qa0, qa1), (qb0, qb1), (fa0, fa1), (fb0, fb1)
    ka, row = lax.axis_index("ka"), lax.axis_index("row")
    z, xh, y = ka // 8, ka // 4 % 2, ka % 4
    xl, core = row // 2, row % 2
    x = xh * 2 + xl

    def device(z_, x_, y_, core_):
        return (z_ * 8 + (x_ // 2) * 4 + y_, (x_ % 2) * 2 + core_)

    sibling = (ka, xl * 2 + 1 - core)
    across = (ka, (1 - xl) * 2 + core)
    diagonal = (ka, (1 - xl) * 2 + 1 - core)
    x_peer = [device(z, (x + d) % 4, y, core) for d in range(1, 4)]
    y_peer = [device(z, x, (y + d) % 4, core) for d in range(1, 4)]
    z_peer = [[device((z + d) % 8, x, y, core if r == 0 else 1 - core) for r in range(2)] for d in range(8)]

    barrier = pltpu.get_barrier_semaphore()
    peers = [sibling, diagonal] + x_peer + y_peer + [z_peer[d][r] for d in range(1, 8) for r in range(2)]
    for peer in peers:
        pl.semaphore_signal(barrier, inc=1, device_id=peer, device_id_type=MESH)

    locals_ = [pltpu.make_async_copy(yz_hbm, yz, lsem.at[0])]
    own_bands = pl.ds(pl.multiple_of(xl * NB, NB), NB)
    their_bands = pl.ds(pl.multiple_of((1 - xl) * NB, NB), NB)
    points = [pl.ds(half * HALF, HALF) for half in range(2)]
    for half in range(2):
        locals_.append(pltpu.make_async_copy(emp_hbm.at[0, own_bands, points[half]], efull.at[0, half], lsem.at[1 + half]))
    for copy in locals_:
        copy.start()

    eye = lax.broadcasted_iota(jnp.int32, (NO, NO), 0) == lax.broadcasted_iota(jnp.int32, (NO, NO), 1)
    levels = jnp.broadcast_to(oe_ref[...].astype(F32), (NO, NO))
    column = jnp.sum(jnp.where(eye, levels, 0.0), axis=1, keepdims=True)
    oe_src[...] = jnp.broadcast_to(column, (NO, 128))
    pl.semaphore_wait(barrier, len(peers))

    sent = []

    def send(src, dst, sends, recvs, index, peer):
        copy = pltpu.make_async_remote_copy(
            src_ref=src, dst_ref=dst, send_sem=sends.at[index], recv_sem=recvs.at[index],
            device_id=peer, device_id_type=MESH,
        )
        copy.start()
        sent.append(copy)
        return copy

    shifts, theirs, beside = [[], []], [], []
    for half in range(2):
        for s in (2, 1, 3):
            shifts[half].append(
                send(occ_hbm.at[0, :, points[half]], shift[half].at[s - 1], zsend, zrecv, half * 3 + s - 1, z_peer[2 * s][0])
            )
        theirs.append(send(emp_hbm.at[0, their_bands, points[half]], efull.at[2, half], gsend, grecv, half, across))
    for s in range(1, 4):
        shifts[1].append(send(oe_src, oe_shift.at[s - 1], zsend, zrecv, 5 + s, z_peer[2 * s][0]))
    for half in range(2):
        beside.append(send(emp_hbm.at[0, own_bands, points[half]], efull.at[1, half], gsend, grecv, 2 + half, sibling))

    def kept(line):
        both = jnp.concatenate([line, line], axis=1)
        return jnp.concatenate([both[:, 64 * block : 64 * block + 64] for block in BLOCKS], axis=1)

    g0, g1, g2 = [
        kept(jnp.where(core == 0, wave_ref[axis, 0:1, :], wave_ref[axis, 1:2, :])) for axis in range(3)
    ]
    flip = jnp.where(g2 < 0, -1, 1)
    group = (flip * g1 + 4) * 5 + flip * g2
    index = lax.broadcasted_iota(jnp.int32, (32, COLS), 0)
    piece = index >> 2
    slot = jnp.where(piece < 4, piece >> 1, 2 + (piece & 1))
    half_of = jnp.where(piece < 4, piece & 1, (piece - 4) >> 1)
    src_core = (core + slot) & 1
    src_xl = (xl + (slot >> 1)) & 1
    plane = (src_xl * 2 + src_core) * 8 + half_of * 4 + (index & 3)
    lane = lax.broadcasted_iota(jnp.int32, (32, COLS), 1)
    is_cos = (lane < 256) | ((lane >= 512) & (lane < 640))
    quarter = jnp.where(is_cos, 0, 8)
    turn = ((g0 * plane - quarter) & 31).astype(F32) * (2.0 * math.pi / 32)
    utab[...] = jnp.cos(turn)
    vtab[...] = jnp.sin(turn) * (-flip).astype(F32)
    chosen = lax.broadcasted_iota(jnp.int32, (64, COLS), 0) == group

    def fill(i, carry):
        u = utab[pl.ds(i, 1), :]
        v = vtab[pl.ds(i, 1), :]
        base = pl.multiple_of(i * 128, 128)
        wtab[pl.ds(base, 64), :] = jnp.where(chosen, u, 0.0).astype(BF16)
        wtab[pl.ds(base + 64, 64), :] = jnp.where(chosen, v, 0.0).astype(BF16)
        return carry

    lax.fori_loop(0, 16, fill, 0)

    steps = [jnp.clip(partner_ref[q, 0] // 16, 1, 3) - 1 for q in range(2)]
    passed, gathers = [], [[], []]

    def pass_on(half):
        theirs[half].wait_recv()
        passed.append(send(efull.at[2, half], efull.at[3, half], gsend, grecv, 4 + half, sibling))

    def select(half):
        for copy in shifts[half]:
            copy.wait_recv()
        for q in range(2):
            osel[half, q] = shift[half][steps[q]]
        gathers[half].append(send(osel.at[half, 1 - core], ofull.at[1, half], gsend, grecv, 6 + half, sibling))
        gathers[half].append(send(osel.at[half, core], ofull.at[2, half], gsend, grecv, 8 + half, across))
        gathers[half].append(send(osel.at[half, 1 - core], ofull.at[3, half], gsend, grecv, 10 + half, diagonal))
        ofull[0, half] = osel[half, core]

    def project(number):
        slot, half = PIECES[number]
        for i in range(4):
            lanes = slice(i * YZ, (i + 1) * YZ)
            e = efull[slot, half, :, lanes].astype(F32)
            o = ofull[slot, half, :, lanes].astype(F32)
            density = jnp.concatenate([(o[v : v + 1] * e).astype(BF16) for v in range(NO)], axis=0)
            part = jnp.dot(density, yz[...], preferred_element_type=F32)
            first = (number * 4 + i) * 128
            ybuf[:, first : first + 128] = part.astype(BF16)

    def gathered(begin, end):
        return jnp.dot(ybuf[:, begin * 512 : end * 512], wtab[begin * 512 : end * 512, :], preferred_element_type=F32)

    pass_on(0)
    select(0)
    lax.fori_loop(16, 32, fill, 0)
    ordering[...] = jnp.where(
        lax.broadcasted_iota(jnp.int32, (COLS, COLS), 0) == order_ref[...], 1.0, 0.0
    ).astype(BF16)
    for copy in locals_:
        copy.wait()
    project(0)
    pass_on(1)
    select(1)

    oe = jnp.where(core == 0, oe_shift[steps[0]], oe_shift[steps[1]])
    pick = lax.broadcasted_iota(jnp.int32, (NB, 2 * NB), 1) == lax.broadcasted_iota(jnp.int32, (NB, 2 * NB), 0) + xl * NB
    ee = jnp.broadcast_to(ee_ref[...].astype(F32), (NB, 2 * NB))
    ee = jnp.sum(jnp.where(pick, ee, 0.0), axis=1, keepdims=True)
    weight = jnp.concatenate([1.0 / (ee - oe[v : v + 1, 0:1]) for v in range(NO)], axis=0)

    project(1)
    for half in range(2):
        beside[half].wait_recv()
        gathers[half][0].wait_recv()
        project(2 + half)
    proj[...] = gathered(0, 4)
    for half in range(2):
        gathers[half][1].wait_recv()
        project(4 + 2 * half)
        gathers[half][2].wait_recv()
        passed[half].wait_recv()
        project(5 + 2 * half)
        if half == 0:
            proj[...] = proj[...] + gathered(4, 6)

    value = (proj[...] + gathered(6, 8)) * (1.0 / (4 * PTS))
    left = value.astype(BF16)
    right[...] = (weight * value).astype(BF16)
    left_t[...] = lax.dot_general(
        ordering[...], left, (((1,), (1,)), ((), ())), preferred_element_type=F32
    ).astype(BF16)

    def a_block(h, x_):
        cols = pl.ds(pl.multiple_of(START[h] + x_ % 2 * WIDE[h], WIDE[h]), WIDE[h])
        return jnp.dot(left_t[pl.ds(pl.multiple_of(x_ // 2 * 192, 192), 192), :], right[:, cols], preferred_element_type=F32)

    def b_block(h, y_):
        rows = pl.ds(pl.multiple_of(384 + y_ * 96, 96), 96)
        return jnp.dot(left_t[rows, :], right[:, START[h] : START[h] + 2 * WIDE[h]], preferred_element_type=F32)

    first_a, first_b, second = [[], []], [[], []], [[], []]
    for h in range(2):
        for d in DIST:
            ga[h][d - 1] = a_block(h, (x + d) % 4).astype(BF16)
            first_a[h].append(send(ga[h].at[d - 1], ra[h].at[d - 1], rsend, rrecv, h * 12 + d - 1, x_peer[d - 1]))
            gb[h][d - 1] = b_block(h, (y + d) % 4).astype(BF16)
            first_b[h].append(send(gb[h].at[d - 1], rb[h].at[d - 1], rsend, rrecv, h * 12 + d + 2, y_peer[d - 1]))
    for h in range(2):
        ta[h][...] = a_block(h, x)
        tb[h][...] = b_block(h, y)

    def sum_first(h):
        for copy in first_a[h]:
            copy.wait_recv()
        total = ta[h][...]
        for d in range(3):
            total = total + ra[h][d].astype(F32)
        ta[h][...] = total
        sa[h][...] = total.astype(BF16)
        for d in DIST:
            rows = pl.ds(pl.multiple_of((y + d) % 4 * 48, 48), 48)
            second[h].append(send(sa[h].at[rows], qa[h].at[d - 1], rsend, rrecv, h * 12 + d + 5, y_peer[d - 1]))
        for copy in first_b[h]:
            copy.wait_recv()
        total = tb[h][...]
        for d in range(3):
            total = total + rb[h][d].astype(F32)
        tb[h][...] = total
        sb[h][...] = total.astype(BF16)
        for d in DIST:
            to = (x + d) % 4
            rows = pl.ds(pl.multiple_of(to // 2 * 48, 48), 48)
            cols = pl.ds(pl.multiple_of(to % 2 * WIDE[h], WIDE[h]), WIDE[h])
            second[h].append(send(sb[h].at[rows, cols], qb[h].at[d - 1], rsend, rrecv, h * 12 + d + 8, x_peer[d - 1]))

    third = [[], []]

    def sum_second(h):
        for copy in second[h]:
            copy.wait_recv()
        total = ta[h][pl.ds(pl.multiple_of(y * 48, 48), 48), :]
        for d in range(3):
            total = total + qa[h][d].astype(F32)
        fa[h][0:48, :] = total
        total = tb[h][pl.ds(pl.multiple_of(xh * 48, 48), 48), pl.ds(pl.multiple_of(xl * WIDE[h], WIDE[h]), WIDE[h])]
        for d in range(3):
            total = total + qb[h][d].astype(F32)
        fb[h][0:48, :] = total
        for to in range(8):
            source = fa[h] if to < 4 else fb[h]
            if h == 0:
                for half in range(2):
                    st0[to, half] = source[to % 4 * 12 : to % 4 * 12 + 16, half * 128 : half * 128 + 128].astype(BF16)
            else:
                st1[to] = source[to % 4 * 12 : to % 4 * 12 + 16, :].astype(BF16)
        for d in (4, 3, 5, 2, 6, 1, 7, 0):
            for r in range(2):
                if d or r:
                    to = (z + d) % 8
                    if h == 0:
                        src, dst = st0.at[to, core if r == 0 else 1 - core], r30.at[d, r]
                    else:
                        src, dst = st1.at[to], r31.at[d, r]
                    third[h].append(send(src, dst, fsend, frecv, h * 16 + d * 2 + r, z_peer[d][r]))

    sum_first(0)
    sum_first(1)
    sum_second(0)
    sum_second(1)

    def sum_third(h):
        for copy in third[h]:
            copy.wait_recv()
        landed = (r30, r31)[h]
        mine = (st0[z, core] if h == 0 else st1[z]).astype(F32)
        other = landed[0, 1].astype(F32)
        for d in range(1, 8):
            mine = mine + landed[d, 0].astype(F32)
            other = other + landed[d, 1].astype(F32)
        first = jnp.where(core == 0, mine, other)[0:12]
        last = jnp.where(core == 0, other, mine)[0:12]
        for q, total in enumerate((first, last)):
            if h == 0:
                out_ref[:, q, 0:128] = total
            else:
                out_ref[:, q, 128:192] = jnp.where(core == 0, total[:, 0:64], total[:, 64:128])

    sum_third(0)
    sum_third(1)
    for copy in sent:
        copy.wait_send()


def per_device(occupied, empty, occ_energy, emp_energy, partner, gvecs):
    waves = jnp.transpose(gvecs, (2, 0, 1))
    vmem = pl.BlockSpec(memory_space=pltpu.VMEM)
    hbm = pl.BlockSpec(memory_space=pl.ANY)
    smem = pl.BlockSpec(memory_space=pltpu.SMEM)
    dma = pltpu.SemaphoreType.DMA

    def chunks(shape, dtype=BF16):
        return [pltpu.VMEM(shape(width), dtype) for width in WIDE]

    out = pl.pallas_call(
        kernel,
        out_shape=jax.ShapeDtypeStruct((12, 2, 192), F32),
        in_specs=[hbm, hbm, vmem, vmem, smem, vmem, vmem, hbm],
        out_specs=vmem,
        scratch_shapes=[
            pltpu.VMEM((3, NO, HALF), BF16),
            pltpu.VMEM((3, NO, HALF), BF16),
            pltpu.VMEM((NO, 128), F32),
            pltpu.VMEM((3, NO, 128), F32),
            pltpu.VMEM((4, 2, NB, HALF), BF16),
            pltpu.VMEM((2, 2, NO, HALF), BF16),
            pltpu.VMEM((4, 2, NO, HALF), BF16),
            pltpu.VMEM((YZ, 128), BF16),
            pltpu.VMEM((4096, COLS), BF16),
            pltpu.VMEM((32, COLS), F32),
            pltpu.VMEM((32, COLS), F32),
            pltpu.VMEM((PAIRS, 4096), BF16),
            pltpu.VMEM((PAIRS, COLS), F32),
            pltpu.VMEM((COLS, COLS), BF16),
            pltpu.VMEM((COLS, PAIRS), BF16),
            pltpu.VMEM((PAIRS, COLS), BF16),
        ]
        + chunks(lambda width: (3, 192, width))
        + chunks(lambda width: (3, 96, 2 * width))
        + chunks(lambda width: (3, 192, width))
        + chunks(lambda width: (3, 96, 2 * width))
        + chunks(lambda width: (192, width), F32)
        + chunks(lambda width: (96, 2 * width), F32)
        + chunks(lambda width: (192, width))
        + chunks(lambda width: (96, 2 * width))
        + chunks(lambda width: (3, 48, width))
        + chunks(lambda width: (3, 48, width))
        + chunks(lambda width: (64, width), F32)
        + chunks(lambda width: (64, width), F32)
        + [
            pltpu.VMEM((8, 2, 16, 128), BF16),
            pltpu.VMEM((8, 16, 128), BF16),
            pltpu.VMEM((8, 2, 16, 128), BF16),
            pltpu.VMEM((8, 2, 16, 128), BF16),
            dma((9,)), dma((9,)), dma((12,)), dma((12,)), dma((24,)), dma((24,)), dma((32,)), dma((32,)), dma((3,)),
        ],
        compiler_params=pltpu.CompilerParams(
            collective_id=0, has_side_effects=True, vmem_limit_bytes=60 * 1024 * 1024
        ),
    )(
        occupied, empty, occ_energy, emp_energy, partner, waves,
        jnp.asarray(row_order()), jnp.asarray(yz_table()).astype(BF16),
    )
    return jnp.swapaxes(out, 0, 1)


def solution(mesh):
    placed = (P("ka", None, "row"), P("ka", None, "row"), P("ka", None), P("ka", None), P(), P())
    return jax.shard_map(
        per_device, mesh=mesh, in_specs=placed, out_specs=P(None, "ka", "row"), check_vma=False
    )
```

```python
import math

import jax
import jax.numpy as jnp
import numpy as np
from jax import lax
from jax.experimental import pallas as pl
from jax.experimental.pallas import tpu as pltpu
from jax.sharding import PartitionSpec as P

MESH = pl.DeviceIdType.MESH
F32 = jnp.float32
BF16 = jnp.bfloat16
NO = 8
NE = 64
NG = 384
PTS = 4096
HALF = PTS // 2
QUART = PTS // 4
YZ = 512
GZ = 32
COLS = 2 * NG
OWN = COLS // 2
PAIRS = NO * NE
BLOCKS = (0, 1, 6, 7, 2, 8, 3, 4, 9, 10, 5, 11)
PIECES = tuple((slot, part) for slot in range(2) for part in range(4)) + tuple(
    (slot, part) for part in range(4) for slot in (2, 3)
)


def yz_table():
    point = np.arange(YZ)
    y, z = point // GZ, point % GZ
    table = np.zeros((YZ, 128), np.float64)
    for g1 in range(-4, 5):
        for g2 in range(5):
            turn = 2 * math.pi * ((g1 * y * 2 + g2 * z) % 32) / 32
            column = (g1 + 4) * 5 + g2
            table[:, column] = np.cos(turn)
            table[:, 64 + column] = np.sin(turn)
    return table.astype(np.float32)


def row_order():
    a = np.concatenate([np.arange(64) + 64 * block for block in BLOCKS])
    z, xh, y, i = a // 96, a // 48 % 2, a // 12 % 4, a % 12
    first = y * 96 + xh * 48 + (z % 4) * 12 + i
    second = 384 + xh * 192 + y * 48 + (z % 4) * 12 + i
    return np.where(z < 4, first, second).astype(np.int32).reshape(1, COLS)


def kernel(
    occ_hbm, emp_hbm, oe_hbm, ee_hbm, partner_hbm, wave_hbm, order_hbm, yz_hbm, out_ref,
    oe_ref, ee_ref, partner_ref, wave_ref, order_ref,
    shift0, shift1, oe_src, oe_shift, efull, osel, ofull, yz, wtab, utab, vtab, ybuf, proj, ordering, left_t, right,
    ga, gb, ra, rb, ta, tb, sa, sb, qa, qb, fa, fb, st, r3,
    zsend, zrecv, gsend, grecv, rsend, rrecv, fsend, frecv, lsem,
):
    shift = (shift0, shift1)
    ka, row = lax.axis_index("ka"), lax.axis_index("row")
    z, xh, y = ka // 8, ka // 4 % 2, ka % 4
    xl, core = row // 2, row % 2

    def device(z_, xh_, y_, xl_, core_):
        return (z_ * 8 + xh_ * 4 + y_, xl_ * 2 + core_)

    sibling = device(z, xh, y, xl, 1 - core)
    beyond = device(z, 1 - xh, y, xl, core)
    y_peer = [device(z, xh, (y + d) % 4, xl, core) for d in range(1, 4)]
    z_peer = [[device((z + d) % 8, xh, y, xl if r == 0 else 1 - xl, core) for r in range(2)] for d in range(8)]
    across = z_peer[0][1]

    barrier = pltpu.get_barrier_semaphore()
    peers = [z_peer[d][r] for d in (4, 3, 5, 2, 6, 1, 7) for r in range(2)] + [beyond] + y_peer + [across, sibling]
    for peer in peers:
        pl.semaphore_signal(barrier, inc=1, device_id=peer, device_id_type=MESH)

    small = []
    for number, (src, dst) in enumerate(
        [(oe_hbm, oe_ref), (wave_hbm, wave_ref), (ee_hbm, ee_ref), (partner_hbm, partner_ref), (order_hbm, order_ref), (yz_hbm, yz)]
    ):
        small.append(pltpu.make_async_copy(src, dst, lsem.at[number]))
    local = []
    points = [pl.ds(part * QUART, QUART) for part in range(4)]
    for part in range(4):
        local.append(pltpu.make_async_copy(emp_hbm.at[0, :, points[part]], efull.at[0, part], lsem.at[6 + part]))
    for copy in small + local:
        copy.start()
    small[0].wait()

    eye = lax.broadcasted_iota(jnp.int32, (NO, NO), 0) == lax.broadcasted_iota(jnp.int32, (NO, NO), 1)
    levels = jnp.broadcast_to(oe_ref[...].astype(F32), (NO, NO))
    column = jnp.sum(jnp.where(eye, levels, 0.0), axis=1, keepdims=True)
    oe_src[...] = jnp.broadcast_to(column, (NO, 128))
    pl.semaphore_wait(barrier, len(peers))

    sent = []

    def send(src, dst, sends, recvs, index, peer):
        copy = pltpu.make_async_remote_copy(
            src_ref=src, dst_ref=dst, send_sem=sends.at[index], recv_sem=recvs.at[index],
            device_id=peer, device_id_type=MESH,
        )
        copy.start()
        sent.append(copy)
        return copy

    shifts, theirs, beside = [[], []], [], []

    def cross(part):
        theirs.append(send(emp_hbm.at[0, :, points[part]], efull.at[2, part], gsend, grecv, part, across))

    for half in range(2):
        for s in (2, 1, 3):
            src = occ_hbm.at[0, :, pl.ds(half * HALF, HALF)]
            shifts[half].append(send(src, shift[half].at[s - 1], zsend, zrecv, half * 3 + s - 1, z_peer[2 * s][0]))
        cross(half)
    for s in range(1, 4):
        shifts[1].append(send(oe_src, oe_shift.at[s - 1], zsend, zrecv, 5 + s, z_peer[2 * s][0]))
    for part in range(4):
        beside.append(send(emp_hbm.at[0, :, points[part]], efull.at[1, part], gsend, grecv, 4 + part, sibling))

    for copy in small[1:]:
        copy.wait()

    def kept(line):
        both = jnp.concatenate([line, line], axis=1)
        return jnp.concatenate([both[:, 64 * block : 64 * block + 64] for block in BLOCKS], axis=1)

    g0, g1, g2 = [
        kept(jnp.where(xl == 0, wave_ref[axis, 0:1, :], wave_ref[axis, 1:2, :])) for axis in range(3)
    ]
    flip = jnp.where(g2 < 0, -1, 1)
    group = (flip * g1 + 4) * 5 + flip * g2
    index = lax.broadcasted_iota(jnp.int32, (32, COLS), 0)
    late = index - 16
    slot_of = jnp.where(index < 16, index >> 3, 2 + ((late >> 1) & 1))
    plane_of = jnp.where(index < 16, index & 7, (late >> 2) * 2 + (late & 1))
    src_core = (core + slot_of) & 1
    src_xl = (xl + (slot_of >> 1)) & 1
    plane = (src_xl * 2 + src_core) * 8 + plane_of
    lane = lax.broadcasted_iota(jnp.int32, (32, COLS), 1)
    lane = jnp.where(lane < OWN, lane, lane - OWN)
    is_cos = (lane < 128) | ((lane >= 256) & (lane < 320))
    turn = ((g0 * plane - jnp.where(is_cos, 0, 8)) & 31).astype(F32) * (2.0 * math.pi / 32)
    utab[...] = jnp.cos(turn)
    vtab[...] = jnp.sin(turn) * (-flip).astype(F32)
    chosen = lax.broadcasted_iota(jnp.int32, (64, COLS), 0) == group

    def fill(i, carry):
        u = utab[pl.ds(i, 1), :]
        v = vtab[pl.ds(i, 1), :]
        base = pl.multiple_of(i * 128, 128)
        wtab[pl.ds(base, 64), :] = jnp.where(chosen, u, 0.0).astype(BF16)
        wtab[pl.ds(base + 64, 64), :] = jnp.where(chosen, v, 0.0).astype(BF16)
        return carry

    steps = [jnp.clip(partner_ref[q, 0] // 16, 1, 3) - 1 for q in range(2)]
    passed, passed_occ, occ_beside, occ_across = [], [], [], []

    def pass_on(part):
        theirs[part].wait_recv()
        passed.append(send(efull.at[2, part], efull.at[3, part], gsend, grecv, 8 + part, sibling))

    def pass_occ(half):
        occ_across[half].wait_recv()
        passed_occ.append(send(ofull.at[2, half], ofull.at[3, half], gsend, grecv, 16 + half, sibling))

    def select(half):
        for copy in shifts[half]:
            copy.wait_recv()
        for q in range(2):
            osel[half, q] = shift[half][steps[q]]
        occ_across.append(send(osel.at[half, 1 - xl], ofull.at[2, half], gsend, grecv, 14 + half, across))
        occ_beside.append(send(osel.at[half, xl], ofull.at[1, half], gsend, grecv, 12 + half, sibling))
        ofull[0, half] = osel[half, xl]

    def project(number):
        slot, part = PIECES[number]
        for i in range(2):
            first = i * YZ
            e = efull[slot, part, :, first : first + YZ]
            first += part % 2 * QUART
            o = ofull[slot, part // 2, :, first : first + YZ]
            density = jnp.concatenate([o[v : v + 1] * e for v in range(NO)], axis=0)
            term = jnp.dot(density, yz[...], preferred_element_type=F32)
            first = (number * 2 + i) * 128
            ybuf[:, first : first + 128] = term.astype(BF16)

    def gathered(begin, end):
        return jnp.dot(ybuf[:, begin * 256 : end * 256], wtab[begin * 256 : end * 256, :], preferred_element_type=F32)

    lax.fori_loop(0, 16, fill, 0)
    select(0)
    cross(2)
    pass_on(0)
    lax.fori_loop(16, 32, fill, 0)
    select(1)
    cross(3)
    pass_occ(0)
    pass_on(1)
    for part in range(4):
        local[part].wait()
        project(part)
    occ_beside[0].wait_recv()
    occ_beside[1].wait_recv()
    for part in range(4):
        beside[part].wait_recv()
        project(4 + part)
    proj[...] = gathered(0, 8)
    pass_occ(1)
    pass_on(2)
    ordering[...] = jnp.where(
        lax.broadcasted_iota(jnp.int32, (COLS, COLS), 0) == order_ref[...], 1.0, 0.0
    ).astype(BF16)

    oe = jnp.where(xl == 0, oe_shift[steps[0]], oe_shift[steps[1]])
    pick = lax.broadcasted_iota(jnp.int32, (NE, NE), 1) == lax.broadcasted_iota(jnp.int32, (NE, NE), 0)
    ee = jnp.broadcast_to(ee_ref[...].astype(F32), (NE, NE))
    ee = jnp.sum(jnp.where(pick, ee, 0.0), axis=1, keepdims=True)
    weight = jnp.concatenate([1.0 / (ee - oe[v : v + 1, 0:1]) for v in range(NO)], axis=0)

    for part in range(4):
        project(8 + 2 * part)
        passed[part].wait_recv()
        if part % 2 == 0:
            passed_occ[part // 2].wait_recv()
        project(9 + 2 * part)
        if part == 1:
            pass_on(3)
        if part < 3:
            proj[...] = proj[...] + gathered(8 + 2 * part, 10 + 2 * part)
    proj[...] = (proj[...] + gathered(14, 16)) * (1.0 / (4 * PTS))
    left = proj[...].astype(BF16)
    right[...] = (weight * proj[:, pl.ds(pl.multiple_of(core * OWN, OWN), OWN)]).astype(BF16)
    left_t[...] = lax.dot_general(
        ordering[...], left, (((1,), (1,)), ((), ())), preferred_element_type=F32
    ).astype(BF16)

    def a_block(y_):
        rows = pl.ds(pl.multiple_of(y_ * 96, 96), 96)
        return jnp.dot(left_t[rows, :], right[...], preferred_element_type=F32)

    def b_block(xh_):
        rows = pl.ds(pl.multiple_of(384 + xh_ * 192, 192), 192)
        return jnp.dot(left_t[rows, :], right[...], preferred_element_type=F32)

    gb[...] = b_block(1 - xh).astype(BF16)
    first_b = send(gb, rb, rsend, rrecv, 3, beyond)
    first_a, second_b = [], []
    for d in (2, 1, 3):
        ga[d - 1] = a_block((y + d) % 4).astype(BF16)
        first_a.append(send(ga.at[d - 1], ra.at[d - 1], rsend, rrecv, d - 1, y_peer[d - 1]))
    ta[...] = a_block(y)
    tb[...] = b_block(xh)

    for copy in first_a:
        copy.wait_recv()
    total = ta[...]
    for d in range(3):
        total = total + ra[d].astype(F32)
    ta[...] = total
    sa[...] = total.astype(BF16)
    rows = pl.ds(pl.multiple_of((1 - xh) * 48, 48), 48)
    second_a = send(sa.at[rows], qa, rsend, rrecv, 4, beyond)
    first_b.wait_recv()
    total = tb[...] + rb[...].astype(F32)
    tb[...] = total
    sb[...] = total.astype(BF16)
    for d in (2, 1, 3):
        rows = pl.ds(pl.multiple_of((y + d) % 4 * 48, 48), 48)
        second_b.append(send(sb.at[rows], qb.at[d - 1], rsend, rrecv, d + 4, y_peer[d - 1]))

    third = {}

    def ready(source, first):
        for to in range(4):
            rows = slice(to * 12, to * 12 + 16)
            tail = source[rows, 256:384].astype(BF16)
            for side in range(2):
                st[first + to, side, :, 0:128] = source[rows, side * 128 : side * 128 + 128].astype(BF16)
                st[first + to, side, :, 128:256] = tail

    second_a.wait_recv()
    fa[0:48, :] = ta[pl.ds(pl.multiple_of(xh * 48, 48), 48), :] + qa[...].astype(F32)
    ready(fa, 0)
    for copy in second_b:
        copy.wait_recv()
    total = tb[pl.ds(pl.multiple_of(y * 48, 48), 48), :]
    for d in range(3):
        total = total + qb[d].astype(F32)
    fb[0:48, :] = total
    ready(fb, 4)
    for d in (4, 3, 5, 2, 6, 1, 7, 0):
        for r in range(2):
            if d or r:
                side = xl if r == 0 else 1 - xl
                third[d, r] = send(st.at[(z + d) % 8, side], r3.at[d, r], fsend, frecv, d * 2 + r, z_peer[d][r])
    mine = st[z, xl].astype(F32)
    other = jnp.zeros((16, 256), F32)
    for d in (0, 1, 7, 2, 6, 3, 5, 4):
        if d:
            third[d, 0].wait_recv()
            mine = mine + r3[d, 0].astype(F32)
        third[d, 1].wait_recv()
        other = other + r3[d, 1].astype(F32)
    for q in range(2):
        total = jnp.where(xl == q, mine, other)[0:12]
        out_ref[q, :, 0:128] = total[:, 0:128]
        out_ref[q, :, 128:192] = jnp.where(xl == 0, total[:, 128:192], total[:, 192:256])
    for copy in sent:
        copy.wait_send()


def per_device(occupied, empty, occ_energy, emp_energy, partner, gvecs):
    waves = jnp.transpose(gvecs, (2, 0, 1))
    hbm = pl.BlockSpec(memory_space=pl.ANY)
    dma = pltpu.SemaphoreType.DMA
    return pl.pallas_call(
        kernel,
        out_shape=jax.ShapeDtypeStruct((2, 12, 192), F32),
        in_specs=[hbm] * 8,
        out_specs=pl.BlockSpec(memory_space=pltpu.VMEM),
        scratch_shapes=[
            pltpu.VMEM((1, NO), BF16),
            pltpu.VMEM((1, NE), BF16),
            pltpu.SMEM((2, 64), jnp.int32),
            pltpu.VMEM((3, 2, NG), jnp.int32),
            pltpu.VMEM((1, COLS), jnp.int32),
            pltpu.VMEM((3, NO, HALF), BF16),
            pltpu.VMEM((3, NO, HALF), BF16),
            pltpu.VMEM((NO, 128), F32),
            pltpu.VMEM((3, NO, 128), F32),
            pltpu.VMEM((4, 4, NE, QUART), BF16),
            pltpu.VMEM((2, 2, NO, HALF), BF16),
            pltpu.VMEM((4, 2, NO, HALF), BF16),
            pltpu.VMEM((YZ, 128), BF16),
            pltpu.VMEM((4096, COLS), BF16),
            pltpu.VMEM((32, COLS), F32),
            pltpu.VMEM((32, COLS), F32),
            pltpu.VMEM((PAIRS, 4096), BF16),
            pltpu.VMEM((PAIRS, COLS), F32),
            pltpu.VMEM((COLS, COLS), BF16),
            pltpu.VMEM((COLS, PAIRS), BF16),
            pltpu.VMEM((PAIRS, OWN), BF16),
            pltpu.VMEM((3, 96, OWN), BF16),
            pltpu.VMEM((192, OWN), BF16),
            pltpu.VMEM((3, 96, OWN), BF16),
            pltpu.VMEM((192, OWN), BF16),
            pltpu.VMEM((96, OWN), F32),
            pltpu.VMEM((192, OWN), F32),
            pltpu.VMEM((96, OWN), BF16),
            pltpu.VMEM((192, OWN), BF16),
            pltpu.VMEM((48, OWN), BF16),
            pltpu.VMEM((3, 48, OWN), BF16),
            pltpu.VMEM((64, OWN), F32),
            pltpu.VMEM((64, OWN), F32),
            pltpu.VMEM((8, 2, 16, 256), BF16),
            pltpu.VMEM((8, 2, 16, 256), BF16),
            dma((9,)), dma((9,)), dma((18,)), dma((18,)), dma((8,)), dma((8,)), dma((16,)), dma((16,)), dma((10,)),
        ],
        compiler_params=pltpu.CompilerParams(
            collective_id=0, has_side_effects=True, vmem_limit_bytes=60 * 1024 * 1024
        ),
    )(
        occupied, empty, occ_energy, emp_energy, partner, waves,
        jnp.asarray(row_order()), jnp.asarray(yz_table()).astype(BF16),
    )


def solution(mesh):
    placed = (P("ka", None, "row"), P("ka", None, "row"), P("ka", None), P("ka", None), P(), P())
    return jax.shard_map(
        per_device, mesh=mesh, in_specs=placed, out_specs=P(None, "ka", "row"), check_vma=False
    )
```

```python
import math

import jax
import jax.numpy as jnp
import numpy as np
from jax import lax
from jax.experimental import pallas as pl
from jax.experimental.pallas import tpu as pltpu
from jax.sharding import PartitionSpec as P

MESH = pl.DeviceIdType.MESH
F32 = jnp.float32
BF16 = jnp.bfloat16
NO = 8
NE = 64
NB = 32
NG = 384
PTS = 4096
HALF = PTS // 2
QUART = PTS // 4
YZ = 512
GZ = 32
COLS = 2 * NG
OWN = COLS // 2
PAIRS = NO * NB
BLOCKS = (0, 1, 6, 7, 2, 8, 3, 4, 9, 10, 5, 11)
PIECES = tuple((slot, part) for slot in range(2) for part in range(4)) + tuple(
    (slot, part) for part in range(4) for slot in (2, 3)
)


def yz_table():
    point = np.arange(YZ)
    y, z = point // GZ, point % GZ
    table = np.zeros((YZ, 128), np.float64)
    for g1 in range(-4, 5):
        for g2 in range(5):
            turn = 2 * math.pi * ((g1 * y * 2 + g2 * z) % 32) / 32
            column = (g1 + 4) * 5 + g2
            table[:, column] = np.cos(turn)
            table[:, 64 + column] = np.sin(turn)
    return table.astype(np.float32)


def row_order():
    a = np.concatenate([np.arange(64) + 64 * block for block in BLOCKS])
    z, xh, y, i = a // 96, a // 48 % 2, a // 12 % 4, a % 12
    first = y * 96 + xh * 48 + (z % 4) * 12 + i
    second = 384 + xh * 192 + y * 48 + (z % 4) * 12 + i
    return np.where(z < 4, first, second).astype(np.int32).reshape(1, COLS)


def kernel(
    occ_hbm, emp_hbm, oe_hbm, ee_hbm, partner_hbm, wave_hbm, order_hbm, yz_hbm, out_ref,
    oe_ref, ee_ref, partner_ref, wave_ref, order_ref,
    shift0, shift1, oe_src, oe_shift, efull, osel, ofull, yz, wtab, utab, vtab, ybuf, proj, ordering, left_t, right, lefts,
    ga, gb, ra, rb, ta, tb, sa, sb, qa, qb, fa, fb, st, r3,
    zsend, zrecv, gsend, grecv, rsend, rrecv, fsend, frecv, esend, erecv, lsem,
):
    shift = (shift0, shift1)
    ka, row = lax.axis_index("ka"), lax.axis_index("row")
    z, xh, y = ka // 8, ka // 4 % 2, ka % 4
    xl, core = row // 2, row % 2

    def device(z_, xh_, y_, xl_, core_):
        return (z_ * 8 + xh_ * 4 + y_, xl_ * 2 + core_)

    sibling = device(z, xh, y, xl, 1 - core)
    diagonal = device(z, xh, y, 1 - xl, 1 - core)
    beyond = device(z, 1 - xh, y, xl, core)
    y_peer = [device(z, xh, (y + d) % 4, xl, core) for d in range(1, 4)]
    z_peer = [[device((z + d) % 8, xh, y, xl if r == 0 else 1 - xl, core) for r in range(2)] for d in range(8)]
    across = z_peer[0][1]

    barrier = pltpu.get_barrier_semaphore()
    peers = [z_peer[d][r] for d in (4, 3, 5, 2, 6, 1, 7) for r in range(2)] + [beyond] + y_peer + [diagonal, across, sibling]
    for peer in peers:
        pl.semaphore_signal(barrier, inc=1, device_id=peer, device_id_type=MESH)

    small = []
    for number, (src, dst) in enumerate(
        [(oe_hbm, oe_ref), (wave_hbm, wave_ref), (ee_hbm, ee_ref), (partner_hbm, partner_ref), (order_hbm, order_ref), (yz_hbm, yz)]
    ):
        small.append(pltpu.make_async_copy(src, dst, lsem.at[number]))
    local = []
    bands = [pl.ds(pl.multiple_of(c * NB, NB), NB) for c in (core, 1 - core)]
    points = [pl.ds(part * QUART, QUART) for part in range(4)]
    for part in range(4):
        local.append(pltpu.make_async_copy(emp_hbm.at[0, bands[0], points[part]], efull.at[0, part], lsem.at[6 + part]))
    for copy in small + local:
        copy.start()
    small[0].wait()

    eye = lax.broadcasted_iota(jnp.int32, (NO, NO), 0) == lax.broadcasted_iota(jnp.int32, (NO, NO), 1)
    levels = jnp.broadcast_to(oe_ref[...].astype(F32), (NO, NO))
    column = jnp.sum(jnp.where(eye, levels, 0.0), axis=1, keepdims=True)
    oe_src[...] = jnp.broadcast_to(column, (NO, 128))
    pl.semaphore_wait(barrier, len(peers))

    sent = []

    def send(src, dst, sends, recvs, index, peer):
        copy = pltpu.make_async_remote_copy(
            src_ref=src, dst_ref=dst, send_sem=sends.at[index], recv_sem=recvs.at[index],
            device_id=peer, device_id_type=MESH,
        )
        copy.start()
        sent.append(copy)
        return copy

    shifts, theirs, oblique, beside = [[], []], [], [], []

    def cross(part):
        theirs.append(send(emp_hbm.at[0, bands[0], points[part]], efull.at[2, part], gsend, grecv, part, across))
        oblique.append(send(emp_hbm.at[0, bands[1], points[part]], efull.at[3, part], gsend, grecv, 8 + part, diagonal))

    for half in range(2):
        for s in (2, 1, 3):
            src = occ_hbm.at[0, :, pl.ds(half * HALF, HALF)]
            shifts[half].append(send(src, shift[half].at[s - 1], zsend, zrecv, half * 3 + s - 1, z_peer[2 * s][0]))
    cross(0)
    cross(1)
    for s in range(1, 4):
        shifts[1].append(send(oe_src, oe_shift.at[s - 1], zsend, zrecv, 5 + s, z_peer[2 * s][0]))
    for part in range(4):
        beside.append(send(emp_hbm.at[0, bands[1], points[part]], efull.at[1, part], gsend, grecv, 4 + part, sibling))

    for copy in small[1:]:
        copy.wait()

    def kept(line):
        both = jnp.concatenate([line, line], axis=1)
        return jnp.concatenate([both[:, 64 * block : 64 * block + 64] for block in BLOCKS], axis=1)

    g0, g1, g2 = [
        kept(jnp.where(xl == 0, wave_ref[axis, 0:1, :], wave_ref[axis, 1:2, :])) for axis in range(3)
    ]
    flip = jnp.where(g2 < 0, -1, 1)
    group = (flip * g1 + 4) * 5 + flip * g2
    index = lax.broadcasted_iota(jnp.int32, (32, COLS), 0)
    late = index - 16
    slot_of = jnp.where(index < 16, index >> 3, 2 + ((late >> 1) & 1))
    plane_of = jnp.where(index < 16, index & 7, (late >> 2) * 2 + (late & 1))
    src_core = (core + slot_of) & 1
    src_xl = (xl + (slot_of >> 1)) & 1
    plane = (src_xl * 2 + src_core) * 8 + plane_of
    lane = lax.broadcasted_iota(jnp.int32, (32, COLS), 1)
    lane = jnp.where(lane < OWN, lane, lane - OWN)
    is_cos = (lane < 128) | ((lane >= 256) & (lane < 320))
    turn = ((g0 * plane - jnp.where(is_cos, 0, 8)) & 31).astype(F32) * (2.0 * math.pi / 32)
    utab[...] = jnp.cos(turn)
    vtab[...] = jnp.sin(turn) * (-flip).astype(F32)
    chosen = lax.broadcasted_iota(jnp.int32, (64, COLS), 0) == group

    def fill(i, carry):
        u = utab[pl.ds(i, 1), :]
        v = vtab[pl.ds(i, 1), :]
        base = pl.multiple_of(i * 128, 128)
        wtab[pl.ds(base, 64), :] = jnp.where(chosen, u, 0.0).astype(BF16)
        wtab[pl.ds(base + 64, 64), :] = jnp.where(chosen, v, 0.0).astype(BF16)
        return carry

    steps = [jnp.clip(partner_ref[q, 0] // 16, 1, 3) - 1 for q in range(2)]
    passed_occ, occ_beside, occ_across = [], [], []

    def pass_occ(half):
        occ_across[half].wait_recv()
        passed_occ.append(send(ofull.at[2, half], ofull.at[3, half], gsend, grecv, 16 + half, sibling))

    def select(half):
        for copy in shifts[half]:
            copy.wait_recv()
        for q in range(2):
            osel[half, q] = shift[half][steps[q]]
        occ_across.append(send(osel.at[half, 1 - xl], ofull.at[2, half], gsend, grecv, 14 + half, across))
        occ_beside.append(send(osel.at[half, xl], ofull.at[1, half], gsend, grecv, 12 + half, sibling))
        ofull[0, half] = osel[half, xl]

    def project(number):
        slot, part = PIECES[number]
        for i in range(2):
            first = i * YZ
            e = efull[slot, part, :, first : first + YZ]
            first += part % 2 * QUART
            o = ofull[slot, part // 2, :, first : first + YZ]
            density = jnp.concatenate([o[v : v + 1] * e for v in range(NO)], axis=0)
            term = jnp.dot(density, yz[...], preferred_element_type=F32)
            first = (number * 2 + i) * 128
            ybuf[:, first : first + 128] = term.astype(BF16)

    def gathered(begin, end):
        return jnp.dot(ybuf[:, begin * 256 : end * 256], wtab[begin * 256 : end * 256, :], preferred_element_type=F32)

    lax.fori_loop(0, 16, fill, 0)
    select(0)
    cross(2)
    lax.fori_loop(16, 32, fill, 0)
    select(1)
    cross(3)
    pass_occ(0)
    for part in range(4):
        local[part].wait()
        project(part)
    occ_beside[0].wait_recv()
    occ_beside[1].wait_recv()
    for part in range(4):
        beside[part].wait_recv()
        project(4 + part)
    proj[...] = gathered(0, 8)
    pass_occ(1)
    ordering[...] = jnp.where(
        lax.broadcasted_iota(jnp.int32, (COLS, COLS), 0) == order_ref[...], 1.0, 0.0
    ).astype(BF16)

    oe = jnp.where(xl == 0, oe_shift[steps[0]], oe_shift[steps[1]])
    ee = jnp.broadcast_to(ee_ref[...].astype(F32), (NB, NE))
    spot = lax.broadcasted_iota(jnp.int32, (NB, NE), 1) - lax.broadcasted_iota(jnp.int32, (NB, NE), 0)
    weights = []
    for c in (core, 1 - core):
        level = jnp.sum(jnp.where(spot == c * NB, ee, 0.0), axis=1, keepdims=True)
        weights.append(jnp.concatenate([1.0 / (level - oe[v : v + 1, 0:1]) for v in range(NO)], axis=0))

    for part in range(4):
        theirs[part].wait_recv()
        project(8 + 2 * part)
        oblique[part].wait_recv()
        if part % 2 == 0:
            passed_occ[part // 2].wait_recv()
        project(9 + 2 * part)
        if part == 1:
            proj[...] = proj[...] + gathered(8, 12)
    exchange = []
    cols = pl.ds(pl.multiple_of(core * OWN, OWN), OWN)
    for part in range(2):
        rows = slice(part * 128, part * 128 + 128)
        last = jnp.dot(ybuf[rows, 3072:4096], wtab[3072:4096, :], preferred_element_type=F32)
        lefts[0, part] = ((proj[rows, :] + last) * (1.0 / (4 * PTS))).astype(BF16)
        exchange.append(send(lefts.at[0, part], lefts.at[1, part], esend, erecv, part, sibling))
    for who in range(2):
        for part in range(2):
            if who:
                exchange[part].wait_recv()
            first = who * PAIRS + part * 128
            weight = weights[who][part * 128 : part * 128 + 128]
            right[first : first + 128, :] = (weight * lefts[who, part, :, cols].astype(F32)).astype(BF16)
            left_t[:, first : first + 128] = lax.dot_general(
                ordering[...], lefts[who, part], (((1,), (1,)), ((), ())), preferred_element_type=F32
            ).astype(BF16)

    def a_block(y_):
        rows = pl.ds(pl.multiple_of(y_ * 96, 96), 96)
        return jnp.dot(left_t[rows, :], right[...], preferred_element_type=F32)

    def b_block(xh_):
        rows = pl.ds(pl.multiple_of(384 + xh_ * 192, 192), 192)
        return jnp.dot(left_t[rows, :], right[...], preferred_element_type=F32)

    gb[...] = b_block(1 - xh).astype(BF16)
    first_b = send(gb, rb, rsend, rrecv, 3, beyond)
    first_a, second_b = [], []
    for d in (2, 1, 3):
        ga[d - 1] = a_block((y + d) % 4).astype(BF16)
        first_a.append(send(ga.at[d - 1], ra.at[d - 1], rsend, rrecv, d - 1, y_peer[d - 1]))
    ta[...] = a_block(y)
    tb[...] = b_block(xh)

    for copy in first_a:
        copy.wait_recv()
    total = ta[...]
    for d in range(3):
        total = total + ra[d].astype(F32)
    ta[...] = total
    sa[...] = total.astype(BF16)
    rows = pl.ds(pl.multiple_of((1 - xh) * 48, 48), 48)
    second_a = send(sa.at[rows], qa, rsend, rrecv, 4, beyond)
    first_b.wait_recv()
    total = tb[...] + rb[...].astype(F32)
    tb[...] = total
    sb[...] = total.astype(BF16)
    for d in (2, 1, 3):
        rows = pl.ds(pl.multiple_of((y + d) % 4 * 48, 48), 48)
        second_b.append(send(sb.at[rows], qb.at[d - 1], rsend, rrecv, d + 4, y_peer[d - 1]))

    third = {}

    def ready(source, first):
        for to in range(4):
            rows = slice(to * 12, to * 12 + 16)
            tail = source[rows, 256:384].astype(BF16)
            for side in range(2):
                st[first + to, side, :, 0:128] = source[rows, side * 128 : side * 128 + 128].astype(BF16)
                st[first + to, side, :, 128:256] = tail

    second_a.wait_recv()
    fa[0:48, :] = ta[pl.ds(pl.multiple_of(xh * 48, 48), 48), :] + qa[...].astype(F32)
    ready(fa, 0)
    for copy in second_b:
        copy.wait_recv()
    total = tb[pl.ds(pl.multiple_of(y * 48, 48), 48), :]
    for d in range(3):
        total = total + qb[d].astype(F32)
    fb[0:48, :] = total
    ready(fb, 4)
    for d in (4, 3, 5, 2, 6, 1, 7, 0):
        for r in range(2):
            if d or r:
                side = xl if r == 0 else 1 - xl
                third[d, r] = send(st.at[(z + d) % 8, side], r3.at[d, r], fsend, frecv, d * 2 + r, z_peer[d][r])
    mine = st[z, xl].astype(F32)
    other = jnp.zeros((16, 256), F32)
    for d in (0, 1, 7, 2, 6, 3, 5, 4):
        if d:
            third[d, 0].wait_recv()
            mine = mine + r3[d, 0].astype(F32)
        third[d, 1].wait_recv()
        other = other + r3[d, 1].astype(F32)
    for q in range(2):
        total = jnp.where(xl == q, mine, other)[0:12]
        out_ref[q, :, 0:128] = total[:, 0:128]
        out_ref[q, :, 128:192] = jnp.where(xl == 0, total[:, 128:192], total[:, 192:256])
    for copy in sent:
        copy.wait_send()


def per_device(occupied, empty, occ_energy, emp_energy, partner, gvecs):
    waves = jnp.transpose(gvecs, (2, 0, 1))
    hbm = pl.BlockSpec(memory_space=pl.ANY)
    dma = pltpu.SemaphoreType.DMA
    return pl.pallas_call(
        kernel,
        out_shape=jax.ShapeDtypeStruct((2, 12, 192), F32),
        in_specs=[hbm] * 8,
        out_specs=pl.BlockSpec(memory_space=pltpu.VMEM),
        scratch_shapes=[
            pltpu.VMEM((1, NO), BF16),
            pltpu.VMEM((1, NE), BF16),
            pltpu.SMEM((2, 64), jnp.int32),
            pltpu.VMEM((3, 2, NG), jnp.int32),
            pltpu.VMEM((1, COLS), jnp.int32),
            pltpu.VMEM((3, NO, HALF), BF16),
            pltpu.VMEM((3, NO, HALF), BF16),
            pltpu.VMEM((NO, 128), F32),
            pltpu.VMEM((3, NO, 128), F32),
            pltpu.VMEM((4, 4, NB, QUART), BF16),
            pltpu.VMEM((2, 2, NO, HALF), BF16),
            pltpu.VMEM((4, 2, NO, HALF), BF16),
            pltpu.VMEM((YZ, 128), BF16),
            pltpu.VMEM((4096, COLS), BF16),
            pltpu.VMEM((32, COLS), F32),
            pltpu.VMEM((32, COLS), F32),
            pltpu.VMEM((PAIRS, 4096), BF16),
            pltpu.VMEM((PAIRS, COLS), F32),
            pltpu.VMEM((COLS, COLS), BF16),
            pltpu.VMEM((COLS, 2 * PAIRS), BF16),
            pltpu.VMEM((2 * PAIRS, OWN), BF16),
            pltpu.VMEM((2, 2, 128, COLS), BF16),
            pltpu.VMEM((3, 96, OWN), BF16),
            pltpu.VMEM((192, OWN), BF16),
            pltpu.VMEM((3, 96, OWN), BF16),
            pltpu.VMEM((192, OWN), BF16),
            pltpu.VMEM((96, OWN), F32),
            pltpu.VMEM((192, OWN), F32),
            pltpu.VMEM((96, OWN), BF16),
            pltpu.VMEM((192, OWN), BF16),
            pltpu.VMEM((48, OWN), BF16),
            pltpu.VMEM((3, 48, OWN), BF16),
            pltpu.VMEM((64, OWN), F32),
            pltpu.VMEM((64, OWN), F32),
            pltpu.VMEM((8, 2, 16, 256), BF16),
            pltpu.VMEM((8, 2, 16, 256), BF16),
            dma((9,)), dma((9,)), dma((18,)), dma((18,)), dma((8,)), dma((8,)), dma((16,)), dma((16,)), dma((2,)), dma((2,)), dma((10,)),
        ],
        compiler_params=pltpu.CompilerParams(
            collective_id=0, has_side_effects=True, vmem_limit_bytes=60 * 1024 * 1024
        ),
    )(
        occupied, empty, occ_energy, emp_energy, partner, waves,
        jnp.asarray(row_order()), jnp.asarray(yz_table()).astype(BF16),
    )


def solution(mesh):
    placed = (P("ka", None, "row"), P("ka", None, "row"), P("ka", None), P("ka", None), P(), P())
    return jax.shard_map(
        per_device, mesh=mesh, in_specs=placed, out_specs=P(None, "ka", "row"), check_vma=False
    )
```

```python
import math

import jax
import jax.numpy as jnp
import numpy as np
from jax import lax
from jax.experimental import pallas as pl
from jax.experimental.pallas import tpu as pltpu
from jax.sharding import PartitionSpec as P

MESH = pl.DeviceIdType.MESH
F32 = jnp.float32
BF16 = jnp.bfloat16
NO = 8
NE = 64
NB = 32
NG = 384
PTS = 4096
HALF = PTS // 2
QUART = PTS // 4
YZ = 512
GZ = 32
COLS = 2 * NG
OWN = COLS // 2
PAIRS = NO * NB
BLOCKS = (0, 1, 6, 7, 2, 8, 3, 4, 9, 10, 5, 11)
PIECES = tuple((slot, part) for slot in range(2) for part in range(4)) + tuple(
    (slot, part) for part in range(4) for slot in (2, 3)
)


def yz_table():
    point = np.arange(YZ)
    y, z = point // GZ, point % GZ
    table = np.zeros((YZ, 128), np.float64)
    for g1 in range(-4, 5):
        for g2 in range(5):
            turn = 2 * math.pi * ((g1 * y * 2 + g2 * z) % 32) / 32
            column = (g1 + 4) * 5 + g2
            table[:, column] = np.cos(turn)
            table[:, 64 + column] = np.sin(turn)
    return table.astype(np.float32)


def row_order():
    a = np.concatenate([np.arange(64) + 64 * block for block in BLOCKS])
    z, xh, y, i = a // 96, a // 48 % 2, a // 12 % 4, a % 12
    first = y * 96 + xh * 48 + (z % 4) * 12 + i
    second = 384 + xh * 192 + y * 48 + (z % 4) * 12 + i
    return np.where(z < 4, first, second).astype(np.int32).reshape(1, COLS)


def kernel(
    occ_hbm, emp_hbm, oe_hbm, ee_hbm, partner_hbm, wave_hbm, order_hbm, yz_hbm, out_ref,
    oe_ref, ee_ref, partner_ref, wave_ref, order_ref,
    shift0, shift1, oe_src, oe_shift, efull, osel, ofull, yz, wtab, utab, vtab, ybuf, proj, ordering, left_t, right, lefts,
    ga, gb, ra, rb, ta, tb, sa, sb, qa, qb, fa, fb, st, r3,
    zsend, zrecv, gsend, grecv, rsend, rrecv, fsend, frecv, esend, erecv, lsem,
):
    shift = (shift0, shift1)
    ka, row = lax.axis_index("ka"), lax.axis_index("row")
    z, xh, y = ka // 8, ka // 4 % 2, ka % 4
    xl, core = row // 2, row % 2

    def device(z_, xh_, y_, xl_, core_):
        return (z_ * 8 + xh_ * 4 + y_, xl_ * 2 + core_)

    sibling = device(z, xh, y, xl, 1 - core)
    diagonal = device(z, xh, y, 1 - xl, 1 - core)
    beyond = device(z, 1 - xh, y, xl, core)
    y_peer = [device(z, xh, (y + d) % 4, xl, core) for d in range(1, 4)]
    z_peer = [[device((z + d) % 8, xh, y, xl if r == 0 else 1 - xl, core) for r in range(2)] for d in range(8)]
    across = z_peer[0][1]

    barrier = pltpu.get_barrier_semaphore()
    peers = [z_peer[d][r] for d in (4, 3, 5, 2, 6, 1, 7) for r in range(2)] + [beyond] + y_peer + [diagonal, across, sibling]
    for peer in peers:
        pl.semaphore_signal(barrier, inc=1, device_id=peer, device_id_type=MESH)

    small = []
    for number, (src, dst) in enumerate(
        [(oe_hbm, oe_ref), (wave_hbm, wave_ref), (ee_hbm, ee_ref), (partner_hbm, partner_ref), (order_hbm, order_ref), (yz_hbm, yz)]
    ):
        small.append(pltpu.make_async_copy(src, dst, lsem.at[number]))
    local = []
    bands = [pl.ds(pl.multiple_of(c * NB, NB), NB) for c in (core, 1 - core)]
    points = [pl.ds(part * QUART, QUART) for part in range(4)]
    for part in range(4):
        local.append(pltpu.make_async_copy(emp_hbm.at[0, bands[0], points[part]], efull.at[0, part], lsem.at[6 + part]))
    for copy in small + local:
        copy.start()
    small[0].wait()

    eye = lax.broadcasted_iota(jnp.int32, (NO, NO), 0) == lax.broadcasted_iota(jnp.int32, (NO, NO), 1)
    levels = jnp.broadcast_to(oe_ref[...].astype(F32), (NO, NO))
    column = jnp.sum(jnp.where(eye, levels, 0.0), axis=1, keepdims=True)
    oe_src[...] = jnp.broadcast_to(column, (NO, 128))
    pl.semaphore_wait(barrier, len(peers))

    sent = []

    def send(src, dst, sends, recvs, index, peer):
        copy = pltpu.make_async_remote_copy(
            src_ref=src, dst_ref=dst, send_sem=sends.at[index], recv_sem=recvs.at[index],
            device_id=peer, device_id_type=MESH,
        )
        copy.start()
        sent.append(copy)
        return copy

    shifts, theirs, oblique, beside = [[], []], [], [], []

    def cross(part):
        theirs.append(send(emp_hbm.at[0, bands[0], points[part]], efull.at[2, part], gsend, grecv, part, across))
        oblique.append(send(emp_hbm.at[0, bands[1], points[part]], efull.at[3, part], gsend, grecv, 8 + part, diagonal))

    for half in range(2):
        for s in (2, 1, 3):
            src = occ_hbm.at[0, :, pl.ds(half * HALF, HALF)]
            shifts[half].append(send(src, shift[half].at[s - 1], zsend, zrecv, half * 3 + s - 1, z_peer[2 * s][0]))
    cross(0)
    cross(1)
    for s in range(1, 4):
        shifts[1].append(send(oe_src, oe_shift.at[s - 1], zsend, zrecv, 5 + s, z_peer[2 * s][0]))
    for part in range(4):
        beside.append(send(emp_hbm.at[0, bands[1], points[part]], efull.at[1, part], gsend, grecv, 4 + part, sibling))

    for copy in small[1:]:
        copy.wait()

    def kept(line):
        both = jnp.concatenate([line, line], axis=1)
        return jnp.concatenate([both[:, 64 * block : 64 * block + 64] for block in BLOCKS], axis=1)

    g0, g1, g2 = [
        kept(jnp.where(xl == 0, wave_ref[axis, 0:1, :], wave_ref[axis, 1:2, :])) for axis in range(3)
    ]
    flip = jnp.where(g2 < 0, -1, 1)
    group = (flip * g1 + 4) * 5 + flip * g2
    index = lax.broadcasted_iota(jnp.int32, (32, COLS), 0)
    late = index - 16
    slot_of = jnp.where(index < 16, index >> 3, 2 + ((late >> 1) & 1))
    plane_of = jnp.where(index < 16, index & 7, (late >> 2) * 2 + (late & 1))
    src_core = (core + slot_of) & 1
    src_xl = (xl + (slot_of >> 1)) & 1
    plane = (src_xl * 2 + src_core) * 8 + plane_of
    lane = lax.broadcasted_iota(jnp.int32, (32, COLS), 1)
    lane = jnp.where(lane < OWN, lane, lane - OWN)
    is_cos = (lane < 128) | ((lane >= 256) & (lane < 320))
    turn = ((g0 * plane - jnp.where(is_cos, 0, 8)) & 31).astype(F32) * (2.0 * math.pi / 32)
    utab[...] = jnp.cos(turn)
    vtab[...] = jnp.sin(turn) * (-flip).astype(F32)
    chosen = lax.broadcasted_iota(jnp.int32, (64, COLS), 0) == group

    def fill(i, carry):
        u = utab[pl.ds(i, 1), :]
        v = vtab[pl.ds(i, 1), :]
        base = pl.multiple_of(i * 128, 128)
        wtab[pl.ds(base, 64), :] = jnp.where(chosen, u, 0.0).astype(BF16)
        wtab[pl.ds(base + 64, 64), :] = jnp.where(chosen, v, 0.0).astype(BF16)
        return carry

    steps = [jnp.clip(partner_ref[q, 0] // 16, 1, 3) - 1 for q in range(2)]
    passed_occ, occ_beside, occ_across = [], [], []

    def pass_occ(half):
        occ_across[half].wait_recv()
        passed_occ.append(send(ofull.at[2, half], ofull.at[3, half], gsend, grecv, 16 + half, sibling))

    def select(half):
        for copy in shifts[half]:
            copy.wait_recv()
        for q in range(2):
            osel[half, q] = shift[half][steps[q]]
        occ_across.append(send(osel.at[half, 1 - xl], ofull.at[2, half], gsend, grecv, 14 + half, across))
        occ_beside.append(send(osel.at[half, xl], ofull.at[1, half], gsend, grecv, 12 + half, sibling))
        ofull[0, half] = osel[half, xl]

    def project(number):
        slot, part = PIECES[number]
        for i in range(2):
            first = i * YZ
            e = efull[slot, part, :, first : first + YZ]
            first += part % 2 * QUART
            o = ofull[slot, part // 2, :, first : first + YZ]
            density = jnp.concatenate([o[v : v + 1] * e for v in range(NO)], axis=0)
            term = jnp.dot(density, yz[...], preferred_element_type=F32)
            first = (number * 2 + i) * 128
            ybuf[:, first : first + 128] = term.astype(BF16)

    def gathered(begin, end):
        return jnp.dot(ybuf[:, begin * 256 : end * 256], wtab[begin * 256 : end * 256, :], preferred_element_type=F32)

    lax.fori_loop(0, 16, fill, 0)
    select(0)
    cross(2)
    lax.fori_loop(16, 32, fill, 0)
    select(1)
    cross(3)
    pass_occ(0)
    for part in range(4):
        local[part].wait()
        project(part)
    occ_beside[0].wait_recv()
    occ_beside[1].wait_recv()
    for part in range(4):
        beside[part].wait_recv()
        project(4 + part)
    proj[...] = gathered(0, 8)
    pass_occ(1)
    ordering[...] = jnp.where(
        lax.broadcasted_iota(jnp.int32, (COLS, COLS), 0) == order_ref[...], 1.0, 0.0
    ).astype(BF16)

    oe = jnp.where(xl == 0, oe_shift[steps[0]], oe_shift[steps[1]])
    ee = jnp.broadcast_to(ee_ref[...].astype(F32), (NB, NE))
    spot = lax.broadcasted_iota(jnp.int32, (NB, NE), 1) - lax.broadcasted_iota(jnp.int32, (NB, NE), 0)
    weights = []
    for c in (core, 1 - core):
        level = jnp.sum(jnp.where(spot == c * NB, ee, 0.0), axis=1, keepdims=True)
        weights.append(jnp.concatenate([1.0 / (level - oe[v : v + 1, 0:1]) for v in range(NO)], axis=0))

    for part in range(4):
        theirs[part].wait_recv()
        project(8 + 2 * part)
        oblique[part].wait_recv()
        if part % 2 == 0:
            passed_occ[part // 2].wait_recv()
        project(9 + 2 * part)
        if part == 1:
            proj[...] = proj[...] + gathered(8, 12)
        if part == 2:
            proj[...] = proj[...] + gathered(12, 14)
    cols = pl.ds(pl.multiple_of(core * OWN, OWN), OWN)
    lefts[0] = ((proj[...] + gathered(14, 16)) * (1.0 / (4 * PTS))).astype(BF16)
    exchange = send(lefts.at[0], lefts.at[1], esend, erecv, 0, sibling)
    for who in range(2):
        if who:
            exchange.wait_recv()
        span = slice(who * PAIRS, who * PAIRS + PAIRS)
        right[span, :] = (weights[who] * lefts[who, :, cols].astype(F32)).astype(BF16)
        left_t[:, span] = lax.dot_general(
            ordering[...], lefts[who], (((1,), (1,)), ((), ())), preferred_element_type=F32
        ).astype(BF16)

    def a_block(y_):
        rows = pl.ds(pl.multiple_of(y_ * 96, 96), 96)
        return jnp.dot(left_t[rows, :], right[...], preferred_element_type=F32)

    def b_block(xh_):
        rows = pl.ds(pl.multiple_of(384 + xh_ * 192, 192), 192)
        return jnp.dot(left_t[rows, :], right[...], preferred_element_type=F32)

    gb[...] = b_block(1 - xh).astype(BF16)
    first_b = send(gb, rb, rsend, rrecv, 3, beyond)
    first_a, second_b = [], []
    for d in (2, 1, 3):
        ga[d - 1] = a_block((y + d) % 4).astype(BF16)
        first_a.append(send(ga.at[d - 1], ra.at[d - 1], rsend, rrecv, d - 1, y_peer[d - 1]))
    ta[...] = a_block(y)
    tb[...] = b_block(xh)

    for copy in first_a:
        copy.wait_recv()
    total = ta[...]
    for d in range(3):
        total = total + ra[d].astype(F32)
    ta[...] = total
    sa[...] = total.astype(BF16)
    rows = pl.ds(pl.multiple_of((1 - xh) * 48, 48), 48)
    second_a = send(sa.at[rows], qa, rsend, rrecv, 4, beyond)
    first_b.wait_recv()
    total = tb[...] + rb[...].astype(F32)
    tb[...] = total
    sb[...] = total.astype(BF16)
    for d in (2, 1, 3):
        rows = pl.ds(pl.multiple_of((y + d) % 4 * 48, 48), 48)
        second_b.append(send(sb.at[rows], qb.at[d - 1], rsend, rrecv, d + 4, y_peer[d - 1]))

    third = {}

    def ready(source, first):
        for to in range(4):
            rows = slice(to * 12, to * 12 + 16)
            tail = source[rows, 256:384].astype(BF16)
            for side in range(2):
                st[first + to, side, :, 0:128] = source[rows, side * 128 : side * 128 + 128].astype(BF16)
                st[first + to, side, :, 128:256] = tail

    second_a.wait_recv()
    fa[0:48, :] = ta[pl.ds(pl.multiple_of(xh * 48, 48), 48), :] + qa[...].astype(F32)
    ready(fa, 0)
    for copy in second_b:
        copy.wait_recv()
    total = tb[pl.ds(pl.multiple_of(y * 48, 48), 48), :]
    for d in range(3):
        total = total + qb[d].astype(F32)
    fb[0:48, :] = total
    ready(fb, 4)
    for d in (4, 3, 5, 2, 6, 1, 7, 0):
        for r in range(2):
            if d or r:
                side = xl if r == 0 else 1 - xl
                third[d, r] = send(st.at[(z + d) % 8, side], r3.at[d, r], fsend, frecv, d * 2 + r, z_peer[d][r])
    mine = st[z, xl].astype(F32)
    other = jnp.zeros((16, 256), F32)
    for d in (0, 1, 7, 2, 6, 3, 5, 4):
        if d:
            third[d, 0].wait_recv()
            mine = mine + r3[d, 0].astype(F32)
        third[d, 1].wait_recv()
        other = other + r3[d, 1].astype(F32)
    for q in range(2):
        total = jnp.where(xl == q, mine, other)[0:12]
        out_ref[q, :, 0:128] = total[:, 0:128]
        out_ref[q, :, 128:192] = jnp.where(xl == 0, total[:, 128:192], total[:, 192:256])
    for copy in sent:
        copy.wait_send()


def per_device(occupied, empty, occ_energy, emp_energy, partner, gvecs):
    waves = jnp.transpose(gvecs, (2, 0, 1))
    hbm = pl.BlockSpec(memory_space=pl.ANY)
    dma = pltpu.SemaphoreType.DMA
    return pl.pallas_call(
        kernel,
        out_shape=jax.ShapeDtypeStruct((2, 12, 192), F32),
        in_specs=[hbm] * 8,
        out_specs=pl.BlockSpec(memory_space=pltpu.VMEM),
        scratch_shapes=[
            pltpu.VMEM((1, NO), BF16),
            pltpu.VMEM((1, NE), BF16),
            pltpu.SMEM((2, 64), jnp.int32),
            pltpu.VMEM((3, 2, NG), jnp.int32),
            pltpu.VMEM((1, COLS), jnp.int32),
            pltpu.VMEM((3, NO, HALF), BF16),
            pltpu.VMEM((3, NO, HALF), BF16),
            pltpu.VMEM((NO, 128), F32),
            pltpu.VMEM((3, NO, 128), F32),
            pltpu.VMEM((4, 4, NB, QUART), BF16),
            pltpu.VMEM((2, 2, NO, HALF), BF16),
            pltpu.VMEM((4, 2, NO, HALF), BF16),
            pltpu.VMEM((YZ, 128), BF16),
            pltpu.VMEM((4096, COLS), BF16),
            pltpu.VMEM((32, COLS), F32),
            pltpu.VMEM((32, COLS), F32),
            pltpu.VMEM((PAIRS, 4096), BF16),
            pltpu.VMEM((PAIRS, COLS), F32),
            pltpu.VMEM((COLS, COLS), BF16),
            pltpu.VMEM((COLS, 2 * PAIRS), BF16),
            pltpu.VMEM((2 * PAIRS, OWN), BF16),
            pltpu.VMEM((2, PAIRS, COLS), BF16),
            pltpu.VMEM((3, 96, OWN), BF16),
            pltpu.VMEM((192, OWN), BF16),
            pltpu.VMEM((3, 96, OWN), BF16),
            pltpu.VMEM((192, OWN), BF16),
            pltpu.VMEM((96, OWN), F32),
            pltpu.VMEM((192, OWN), F32),
            pltpu.VMEM((96, OWN), BF16),
            pltpu.VMEM((192, OWN), BF16),
            pltpu.VMEM((48, OWN), BF16),
            pltpu.VMEM((3, 48, OWN), BF16),
            pltpu.VMEM((64, OWN), F32),
            pltpu.VMEM((64, OWN), F32),
            pltpu.VMEM((8, 2, 16, 256), BF16),
            pltpu.VMEM((8, 2, 16, 256), BF16),
            dma((9,)), dma((9,)), dma((18,)), dma((18,)), dma((8,)), dma((8,)), dma((16,)), dma((16,)), dma((1,)), dma((1,)), dma((10,)),
        ],
        compiler_params=pltpu.CompilerParams(
            collective_id=0, has_side_effects=True, vmem_limit_bytes=60 * 1024 * 1024
        ),
    )(
        occupied, empty, occ_energy, emp_energy, partner, waves,
        jnp.asarray(row_order()), jnp.asarray(yz_table()).astype(BF16),
    )


def solution(mesh):
    placed = (P("ka", None, "row"), P("ka", None, "row"), P("ka", None), P("ka", None), P(), P())
    return jax.shard_map(
        per_device, mesh=mesh, in_specs=placed, out_specs=P(None, "ka", "row"), check_vma=False
    )
```

```python
import math

import jax
import jax.numpy as jnp
import numpy as np
from jax import lax
from jax.experimental import pallas as pl
from jax.experimental.pallas import tpu as pltpu
from jax.sharding import PartitionSpec as P

MESH = pl.DeviceIdType.MESH
F32 = jnp.float32
BF16 = jnp.bfloat16
NO = 8
NB = 32
NG = 384
PTS = 4096
HALF = PTS // 2
YZ = 512
GZ = 32
COLS = 2 * NG
PAIRS = NO * NB
OWN = COLS // 2
BLOCKS = (0, 1, 3, 4, 2, 5, 6, 7, 9, 10, 8, 11)
PIECES = ((0, 0), (0, 1), (1, 0), (1, 1), (2, 0), (3, 0), (2, 1), (3, 1))
DIST = (2, 1, 3)


def yz_table():
    point = np.arange(YZ)
    y, z = point // GZ, point % GZ
    table = np.zeros((YZ, 128), np.float64)
    for g1 in range(-4, 5):
        for g2 in range(5):
            turn = 2 * math.pi * ((g1 * y * 2 + g2 * z) % 32) / 32
            column = (g1 + 4) * 5 + g2
            table[:, column] = np.cos(turn)
            table[:, 64 + column] = np.sin(turn)
    return table.astype(np.float32)


def row_order():
    a = np.concatenate([np.arange(64) + 64 * block for block in BLOCKS])
    z, xh, y, i = a // 96, a // 48 % 2, a // 12 % 4, a % 12
    first = xh * 192 + y * 48 + (z % 4) * 12 + i
    second = 384 + y * 96 + xh * 48 + (z % 4) * 12 + i
    return np.where(z < 4, first, second).astype(np.int32).reshape(1, COLS)


def kernel(
    occ_hbm, emp_hbm, oe_hbm, ee_hbm, partner_hbm, wave_hbm, order_hbm, yz_hbm, out_ref,
    oe_ref, ee_ref, partner_ref, wave_ref, order_ref,
    shift0, shift1, oe_src, oe_shift, efull, osel, ofull, yz, wtab, utab, vtab, ybuf, proj, ordering, left_t, right,
    ga, gb, ra, rb, ta, tb, sa, sb, qa, qb, fa, fb, st, r3,
    zsend, zrecv, gsend, grecv, rsend, rrecv, fsend, frecv, lsem,
):
    shift = (shift0, shift1)
    ka, row = lax.axis_index("ka"), lax.axis_index("row")
    z, xh, y = ka // 8, ka // 4 % 2, ka % 4
    xl, core = row // 2, row % 2
    x = xh * 2 + xl

    def device(z_, x_, y_, core_):
        return (z_ * 8 + (x_ // 2) * 4 + y_, (x_ % 2) * 2 + core_)

    sibling = (ka, xl * 2 + 1 - core)
    across = (ka, (1 - xl) * 2 + core)
    diagonal = (ka, (1 - xl) * 2 + 1 - core)
    x_peer = [device(z, (x + d) % 4, y, core) for d in range(1, 4)]
    y_peer = [device(z, x, (y + d) % 4, core) for d in range(1, 4)]
    z_peer = [[device((z + d) % 8, x, y, core if r == 0 else 1 - core) for r in range(2)] for d in range(8)]

    barrier = pltpu.get_barrier_semaphore()
    peers = [sibling, diagonal] + x_peer + y_peer + [z_peer[d][r] for d in range(1, 8) for r in range(2)]
    for peer in peers:
        pl.semaphore_signal(barrier, inc=1, device_id=peer, device_id_type=MESH)

    small = []
    for number, (src, dst) in enumerate(
        [(oe_hbm, oe_ref), (wave_hbm, wave_ref), (ee_hbm, ee_ref), (partner_hbm, partner_ref), (order_hbm, order_ref), (yz_hbm, yz)]
    ):
        small.append(pltpu.make_async_copy(src, dst, lsem.at[number]))
    local = []
    own_bands = pl.ds(pl.multiple_of(xl * NB, NB), NB)
    their_bands = pl.ds(pl.multiple_of((1 - xl) * NB, NB), NB)
    points = [pl.ds(half * HALF, HALF) for half in range(2)]
    for half in range(2):
        local.append(pltpu.make_async_copy(emp_hbm.at[0, own_bands, points[half]], efull.at[0, half], lsem.at[6 + half]))
    for copy in small + local:
        copy.start()
    small[0].wait()

    eye = lax.broadcasted_iota(jnp.int32, (NO, NO), 0) == lax.broadcasted_iota(jnp.int32, (NO, NO), 1)
    levels = jnp.broadcast_to(oe_ref[...].astype(F32), (NO, NO))
    column = jnp.sum(jnp.where(eye, levels, 0.0), axis=1, keepdims=True)
    oe_src[...] = jnp.broadcast_to(column, (NO, 128))
    pl.semaphore_wait(barrier, len(peers))

    sent = []

    def send(src, dst, sends, recvs, index, peer):
        copy = pltpu.make_async_remote_copy(
            src_ref=src, dst_ref=dst, send_sem=sends.at[index], recv_sem=recvs.at[index],
            device_id=peer, device_id_type=MESH,
        )
        copy.start()
        sent.append(copy)
        return copy

    shifts, theirs, beside = [[], []], [], []
    for half in range(2):
        for s in (2, 1, 3):
            shifts[half].append(
                send(occ_hbm.at[0, :, points[half]], shift[half].at[s - 1], zsend, zrecv, half * 3 + s - 1, z_peer[2 * s][0])
            )
        theirs.append(send(emp_hbm.at[0, their_bands, points[half]], efull.at[2, half], gsend, grecv, half, across))
    for s in range(1, 4):
        shifts[1].append(send(oe_src, oe_shift.at[s - 1], zsend, zrecv, 5 + s, z_peer[2 * s][0]))
    for half in range(2):
        beside.append(send(emp_hbm.at[0, own_bands, points[half]], efull.at[1, half], gsend, grecv, 2 + half, sibling))

    for copy in small[1:]:
        copy.wait()

    def kept(line):
        both = jnp.concatenate([line, line], axis=1)
        return jnp.concatenate([both[:, 64 * block : 64 * block + 64] for block in BLOCKS], axis=1)

    g0, g1, g2 = [
        kept(jnp.where(core == 0, wave_ref[axis, 0:1, :], wave_ref[axis, 1:2, :])) for axis in range(3)
    ]
    flip = jnp.where(g2 < 0, -1, 1)
    group = (flip * g1 + 4) * 5 + flip * g2
    index = lax.broadcasted_iota(jnp.int32, (32, COLS), 0)
    piece = index >> 2
    slot = jnp.where(piece < 4, piece >> 1, 2 + (piece & 1))
    half_of = jnp.where(piece < 4, piece & 1, (piece - 4) >> 1)
    src_core = (core + slot) & 1
    src_xl = (xl + (slot >> 1)) & 1
    plane = (src_xl * 2 + src_core) * 8 + half_of * 4 + (index & 3)
    lane = lax.broadcasted_iota(jnp.int32, (32, COLS), 1)
    quarter = jnp.where(lane < OWN, 0, 8)
    turn = ((g0 * plane - quarter) & 31).astype(F32) * (2.0 * math.pi / 32)
    utab[...] = jnp.cos(turn)
    vtab[...] = jnp.sin(turn) * (-flip).astype(F32)
    chosen = lax.broadcasted_iota(jnp.int32, (64, COLS), 0) == group

    def fill(i, carry):
        u = utab[pl.ds(i, 1), :]
        v = vtab[pl.ds(i, 1), :]
        base = pl.multiple_of(i * 128, 128)
        wtab[pl.ds(base, 64), :] = jnp.where(chosen, u, 0.0).astype(BF16)
        wtab[pl.ds(base + 64, 64), :] = jnp.where(chosen, v, 0.0).astype(BF16)
        return carry

    lax.fori_loop(0, 32, fill, 0)

    steps = [jnp.clip(partner_ref[q, 0] // 16, 1, 3) - 1 for q in range(2)]
    passed, gathers = [], [[], []]

    def pass_on(half):
        theirs[half].wait_recv()
        passed.append(send(efull.at[2, half], efull.at[3, half], gsend, grecv, 4 + half, sibling))

    def select(half):
        for copy in shifts[half]:
            copy.wait_recv()
        for q in range(2):
            osel[half, q] = shift[half][steps[q]]
        gathers[half].append(send(osel.at[half, 1 - core], ofull.at[1, half], gsend, grecv, 6 + half, sibling))
        gathers[half].append(send(osel.at[half, core], ofull.at[2, half], gsend, grecv, 8 + half, across))
        gathers[half].append(send(osel.at[half, 1 - core], ofull.at[3, half], gsend, grecv, 10 + half, diagonal))
        ofull[0, half] = osel[half, core]

    def project(number):
        slot, half = PIECES[number]
        for i in range(4):
            lanes = slice(i * YZ, (i + 1) * YZ)
            e = efull[slot, half, :, lanes].astype(F32)
            o = ofull[slot, half, :, lanes].astype(F32)
            density = jnp.concatenate([(o[v : v + 1] * e).astype(BF16) for v in range(NO)], axis=0)
            part = jnp.dot(density, yz[...], preferred_element_type=F32)
            first = (number * 4 + i) * 128
            ybuf[:, first : first + 128] = part.astype(BF16)

    def gathered(begin, end):
        return jnp.dot(ybuf[:, begin * 512 : end * 512], wtab[begin * 512 : end * 512, :], preferred_element_type=F32)

    pass_on(0)
    select(0)
    ordering[...] = jnp.where(
        lax.broadcasted_iota(jnp.int32, (COLS, COLS), 0) == order_ref[...], 1.0, 0.0
    ).astype(BF16)
    pass_on(1)
    select(1)

    oe = jnp.where(core == 0, oe_shift[steps[0]], oe_shift[steps[1]])
    pick = lax.broadcasted_iota(jnp.int32, (NB, 2 * NB), 1) == lax.broadcasted_iota(jnp.int32, (NB, 2 * NB), 0) + xl * NB
    ee = jnp.broadcast_to(ee_ref[...].astype(F32), (NB, 2 * NB))
    ee = jnp.sum(jnp.where(pick, ee, 0.0), axis=1, keepdims=True)
    weight = jnp.concatenate([1.0 / (ee - oe[v : v + 1, 0:1]) for v in range(NO)], axis=0)

    for half in range(2):
        local[half].wait()
        project(half)
    for half in range(2):
        beside[half].wait_recv()
        gathers[half][0].wait_recv()
        project(2 + half)
    proj[...] = gathered(0, 4)
    for half in range(2):
        gathers[half][1].wait_recv()
        project(4 + 2 * half)
        gathers[half][2].wait_recv()
        passed[half].wait_recv()
        project(5 + 2 * half)
        if half == 0:
            proj[...] = proj[...] + gathered(4, 6)

    value = (proj[...] + gathered(6, 8)) * (1.0 / (4 * PTS))
    left = value.astype(BF16)
    right[...] = (weight * value).astype(BF16)
    left_t[...] = lax.dot_general(
        ordering[...], left, (((1,), (1,)), ((), ())), preferred_element_type=F32
    ).astype(BF16)

    def a_block(x_):
        rows = pl.ds(pl.multiple_of(x_ // 2 * 192, 192), 192)
        cols = pl.ds(pl.multiple_of(x_ % 2 * OWN, OWN), OWN)
        return jnp.dot(left_t[rows, :], right[:, cols], preferred_element_type=F32)

    def b_block(y_):
        rows = pl.ds(pl.multiple_of(384 + y_ * 96, 96), 96)
        return jnp.dot(left_t[rows, :], right[...], preferred_element_type=F32)

    first_a, first_b, second_a, second_b = [], [], [], []
    for d in DIST:
        ga[d - 1] = a_block((x + d) % 4).astype(BF16)
        first_a.append(send(ga.at[d - 1], ra.at[d - 1], rsend, rrecv, d - 1, x_peer[d - 1]))
        gb[d - 1] = b_block((y + d) % 4).astype(BF16)
        first_b.append(send(gb.at[d - 1], rb.at[d - 1], rsend, rrecv, d + 2, y_peer[d - 1]))
    ta[...] = a_block(x)
    tb[...] = b_block(y)

    for copy in first_a:
        copy.wait_recv()
    total = ta[...]
    for d in range(3):
        total = total + ra[d].astype(F32)
    ta[...] = total
    sa[...] = total.astype(BF16)
    for d in DIST:
        rows = pl.ds(pl.multiple_of((y + d) % 4 * 48, 48), 48)
        second_a.append(send(sa.at[rows], qa.at[d - 1], rsend, rrecv, d + 5, y_peer[d - 1]))
    for copy in first_b:
        copy.wait_recv()
    total = tb[...]
    for d in range(3):
        total = total + rb[d].astype(F32)
    tb[...] = total
    sb[...] = total.astype(BF16)
    for d in DIST:
        to = (x + d) % 4
        rows = pl.ds(pl.multiple_of(to // 2 * 48, 48), 48)
        cols = pl.ds(pl.multiple_of(to % 2 * OWN, OWN), OWN)
        second_b.append(send(sb.at[rows, cols], qb.at[d - 1], rsend, rrecv, d + 8, x_peer[d - 1]))

    third = {}

    def ready(source, first):
        for to in range(4):
            rows = slice(to * 12, to * 12 + 16)
            tail = source[rows, 256:384].astype(BF16)
            for side in range(2):
                st[first + to, side, :, 0:128] = source[rows, side * 128 : side * 128 + 128].astype(BF16)
                st[first + to, side, :, 128:256] = tail

    for copy in second_a:
        copy.wait_recv()
    total = ta[pl.ds(pl.multiple_of(y * 48, 48), 48), :]
    for d in range(3):
        total = total + qa[d].astype(F32)
    fa[0:48, :] = total
    ready(fa, 0)
    for copy in second_b:
        copy.wait_recv()
    total = tb[pl.ds(pl.multiple_of(xh * 48, 48), 48), pl.ds(pl.multiple_of(xl * OWN, OWN), OWN)]
    for d in range(3):
        total = total + qb[d].astype(F32)
    fb[0:48, :] = total
    ready(fb, 4)
    for d in (4, 3, 5, 2, 6, 1, 7, 0):
        for r in range(2):
            if d or r:
                side = core if r == 0 else 1 - core
                third[d, r] = send(st.at[(z + d) % 8, side], r3.at[d, r], fsend, frecv, d * 2 + r, z_peer[d][r])
    mine = st[z, core].astype(F32)
    other = jnp.zeros((16, 256), F32)
    for d in (0, 1, 7, 2, 6, 3, 5, 4):
        if d:
            third[d, 0].wait_recv()
            mine = mine + r3[d, 0].astype(F32)
        third[d, 1].wait_recv()
        other = other + r3[d, 1].astype(F32)
    for q in range(2):
        total = jnp.where(core == q, mine, other)[0:12]
        out_ref[q, :, 0:128] = total[:, 0:128]
        out_ref[q, :, 128:192] = jnp.where(core == 0, total[:, 128:192], total[:, 192:256])
    for copy in sent:
        copy.wait_send()


def per_device(occupied, empty, occ_energy, emp_energy, partner, gvecs):
    waves = jnp.transpose(gvecs, (2, 0, 1))
    hbm = pl.BlockSpec(memory_space=pl.ANY)
    dma = pltpu.SemaphoreType.DMA
    return pl.pallas_call(
        kernel,
        out_shape=jax.ShapeDtypeStruct((2, 12, 192), F32),
        in_specs=[hbm] * 8,
        out_specs=pl.BlockSpec(memory_space=pltpu.VMEM),
        scratch_shapes=[
            pltpu.VMEM((1, NO), BF16),
            pltpu.VMEM((1, 2 * NB), BF16),
            pltpu.SMEM((2, 64), jnp.int32),
            pltpu.VMEM((3, 2, NG), jnp.int32),
            pltpu.VMEM((1, COLS), jnp.int32),
            pltpu.VMEM((3, NO, HALF), BF16),
            pltpu.VMEM((3, NO, HALF), BF16),
            pltpu.VMEM((NO, 128), F32),
            pltpu.VMEM((3, NO, 128), F32),
            pltpu.VMEM((4, 2, NB, HALF), BF16),
            pltpu.VMEM((2, 2, NO, HALF), BF16),
            pltpu.VMEM((4, 2, NO, HALF), BF16),
            pltpu.VMEM((YZ, 128), BF16),
            pltpu.VMEM((4096, COLS), BF16),
            pltpu.VMEM((32, COLS), F32),
            pltpu.VMEM((32, COLS), F32),
            pltpu.VMEM((PAIRS, 4096), BF16),
            pltpu.VMEM((PAIRS, COLS), F32),
            pltpu.VMEM((COLS, COLS), BF16),
            pltpu.VMEM((COLS, PAIRS), BF16),
            pltpu.VMEM((PAIRS, COLS), BF16),
            pltpu.VMEM((3, 192, OWN), BF16),
            pltpu.VMEM((3, 96, COLS), BF16),
            pltpu.VMEM((3, 192, OWN), BF16),
            pltpu.VMEM((3, 96, COLS), BF16),
            pltpu.VMEM((192, OWN), F32),
            pltpu.VMEM((96, COLS), F32),
            pltpu.VMEM((192, OWN), BF16),
            pltpu.VMEM((96, COLS), BF16),
            pltpu.VMEM((3, 48, OWN), BF16),
            pltpu.VMEM((3, 48, OWN), BF16),
            pltpu.VMEM((64, OWN), F32),
            pltpu.VMEM((64, OWN), F32),
            pltpu.VMEM((8, 2, 16, 256), BF16),
            pltpu.VMEM((8, 2, 16, 256), BF16),
            dma((9,)), dma((9,)), dma((12,)), dma((12,)), dma((12,)), dma((12,)), dma((16,)), dma((16,)), dma((8,)),
        ],
        compiler_params=pltpu.CompilerParams(
            collective_id=0, has_side_effects=True, vmem_limit_bytes=60 * 1024 * 1024
        ),
    )(
        occupied, empty, occ_energy, emp_energy, partner, waves,
        jnp.asarray(row_order()), jnp.asarray(yz_table()).astype(BF16),
    )


def solution(mesh):
    placed = (P("ka", None, "row"), P("ka", None, "row"), P("ka", None), P("ka", None), P(), P())
    return jax.shard_map(
        per_device, mesh=mesh, in_specs=placed, out_specs=P(None, "ka", "row"), check_vma=False
    )
```

```python
import math

import jax
import jax.numpy as jnp
import numpy as np
from jax import lax
from jax.experimental import pallas as pl
from jax.experimental.pallas import tpu as pltpu
from jax.sharding import PartitionSpec as P

MESH = pl.DeviceIdType.MESH
F32 = jnp.float32
BF16 = jnp.bfloat16
NO = 8
NE = 64
NB = 32
NG = 384
PTS = 4096
HALF = PTS // 2
QUART = PTS // 4
YZ = 512
GZ = 32
COLS = 2 * NG
OWN = COLS // 2
PAIRS = NO * NB
BLOCKS = (0, 1, 6, 7, 2, 8, 3, 4, 9, 10, 5, 11)
PIECES = tuple((slot, part) for slot in range(2) for part in range(4)) + tuple(
    (slot, part) for part in range(4) for slot in (2, 3)
)


def yz_table():
    point = np.arange(YZ)
    y, z = point // GZ, point % GZ
    table = np.zeros((YZ, 128), np.float64)
    for g1 in range(-4, 5):
        for g2 in range(5):
            turn = 2 * math.pi * ((g1 * y * 2 + g2 * z) % 32) / 32
            column = (g1 + 4) * 5 + g2
            table[:, column] = np.cos(turn)
            table[:, 64 + column] = np.sin(turn)
    return table.astype(np.float32)


def row_order():
    a = np.concatenate([np.arange(64) + 64 * block for block in BLOCKS])
    z, xh, y, i = a // 96, a // 48 % 2, a // 12 % 4, a % 12
    first = y * 96 + xh * 48 + (z % 4) * 12 + i
    second = 384 + xh * 192 + y * 48 + (z % 4) * 12 + i
    return np.where(z < 4, first, second).astype(np.int32).reshape(1, COLS)


def kernel(
    occ_hbm, emp_hbm, oe_hbm, ee_hbm, partner_hbm, wave_hbm, order_hbm, yz_hbm, out_ref,
    oe_ref, ee_ref, partner_ref, wave_ref, order_ref,
    shift0, shift1, oe_src, oe_shift, efull, osel, ofull, yz, wtab, utab, vtab, ybuf, proj, ordering, left_t, right, lefts,
    ga, gb, ra, rb, ta, tb, sa, sb, qa, qb, fa, fb, st, r3,
    zsend, zrecv, gsend, grecv, rsend, rrecv, fsend, frecv, esend, erecv, lsem,
):
    shift = (shift0, shift1)
    ka, row = lax.axis_index("ka"), lax.axis_index("row")
    z, xh, y = ka // 8, ka // 4 % 2, ka % 4
    xl, core = row // 2, row % 2

    def device(z_, xh_, y_, xl_, core_):
        return (z_ * 8 + xh_ * 4 + y_, xl_ * 2 + core_)

    sibling = device(z, xh, y, xl, 1 - core)
    diagonal = device(z, xh, y, 1 - xl, 1 - core)
    beyond = device(z, 1 - xh, y, xl, core)
    y_peer = [device(z, xh, (y + d) % 4, xl, core) for d in range(1, 4)]
    z_peer = [[device((z + d) % 8, xh, y, xl if r == 0 else 1 - xl, core) for r in range(2)] for d in range(8)]
    across = z_peer[0][1]

    barrier = pltpu.get_barrier_semaphore()
    peers = [z_peer[d][r] for d in (4, 3, 5, 2, 6, 1, 7) for r in range(2)] + [beyond] + y_peer + [diagonal, across, sibling]
    for peer in peers:
        pl.semaphore_signal(barrier, inc=1, device_id=peer, device_id_type=MESH)

    small = []
    for number, (src, dst) in enumerate(
        [(oe_hbm, oe_ref), (wave_hbm, wave_ref), (ee_hbm, ee_ref), (partner_hbm, partner_ref), (order_hbm, order_ref), (yz_hbm, yz)]
    ):
        small.append(pltpu.make_async_copy(src, dst, lsem.at[number]))
    local = []
    bands = [pl.ds(pl.multiple_of(c * NB, NB), NB) for c in (core, 1 - core)]
    points = [pl.ds(part * QUART, QUART) for part in range(4)]
    for part in range(4):
        local.append(pltpu.make_async_copy(emp_hbm.at[0, bands[0], points[part]], efull.at[0, part], lsem.at[6 + part]))
    for copy in small + local:
        copy.start()
    small[0].wait()

    eye = lax.broadcasted_iota(jnp.int32, (NO, NO), 0) == lax.broadcasted_iota(jnp.int32, (NO, NO), 1)
    levels = jnp.broadcast_to(oe_ref[...].astype(F32), (NO, NO))
    column = jnp.sum(jnp.where(eye, levels, 0.0), axis=1, keepdims=True)
    oe_src[...] = jnp.broadcast_to(column, (NO, 128))
    pl.semaphore_wait(barrier, len(peers))

    sent = []

    def send(src, dst, sends, recvs, index, peer):
        copy = pltpu.make_async_remote_copy(
            src_ref=src, dst_ref=dst, send_sem=sends.at[index], recv_sem=recvs.at[index],
            device_id=peer, device_id_type=MESH,
        )
        copy.start()
        sent.append(copy)
        return copy

    shifts, theirs, oblique, beside = [[], []], [], [], []

    def cross(part):
        theirs.append(send(emp_hbm.at[0, bands[0], points[part]], efull.at[2, part], gsend, grecv, part, across))
        oblique.append(send(emp_hbm.at[0, bands[1], points[part]], efull.at[3, part], gsend, grecv, 8 + part, diagonal))

    for half in range(2):
        for s in (2, 1, 3):
            src = occ_hbm.at[0, :, pl.ds(half * HALF, HALF)]
            shifts[half].append(send(src, shift[half].at[s - 1], zsend, zrecv, half * 3 + s - 1, z_peer[2 * s][0]))
    cross(0)
    cross(1)
    for s in range(1, 4):
        shifts[1].append(send(oe_src, oe_shift.at[s - 1], zsend, zrecv, 5 + s, z_peer[2 * s][0]))
    for part in range(4):
        beside.append(send(emp_hbm.at[0, bands[1], points[part]], efull.at[1, part], gsend, grecv, 4 + part, sibling))

    for copy in small[1:]:
        copy.wait()

    def kept(line):
        both = jnp.concatenate([line, line], axis=1)
        return jnp.concatenate([both[:, 64 * block : 64 * block + 64] for block in BLOCKS], axis=1)

    g0, g1, g2 = [
        kept(jnp.where(xl == 0, wave_ref[axis, 0:1, :], wave_ref[axis, 1:2, :])) for axis in range(3)
    ]
    flip = jnp.where(g2 < 0, -1, 1)
    group = (flip * g1 + 4) * 5 + flip * g2
    index = lax.broadcasted_iota(jnp.int32, (32, COLS), 0)
    late = index - 16
    slot_of = jnp.where(index < 16, index >> 3, 2 + ((late >> 1) & 1))
    plane_of = jnp.where(index < 16, index & 7, (late >> 2) * 2 + (late & 1))
    src_core = (core + slot_of) & 1
    src_xl = (xl + (slot_of >> 1)) & 1
    plane = (src_xl * 2 + src_core) * 8 + plane_of
    lane = lax.broadcasted_iota(jnp.int32, (32, COLS), 1)
    lane = jnp.where(lane < OWN, lane, lane - OWN)
    is_cos = (lane < 128) | ((lane >= 256) & (lane < 320))
    turn = ((g0 * plane - jnp.where(is_cos, 0, 8)) & 31).astype(F32) * (2.0 * math.pi / 32)
    utab[...] = jnp.cos(turn)
    vtab[...] = jnp.sin(turn) * (-flip).astype(F32)
    chosen = lax.broadcasted_iota(jnp.int32, (64, COLS), 0) == group

    def fill(i, carry):
        u = utab[pl.ds(i, 1), :]
        v = vtab[pl.ds(i, 1), :]
        base = pl.multiple_of(i * 128, 128)
        wtab[pl.ds(base, 64), :] = jnp.where(chosen, u, 0.0).astype(BF16)
        wtab[pl.ds(base + 64, 64), :] = jnp.where(chosen, v, 0.0).astype(BF16)
        return carry

    steps = [jnp.clip(partner_ref[q, 0] // 16, 1, 3) - 1 for q in range(2)]
    passed_occ, occ_beside, occ_across = [], [], []

    def select(half):
        for copy in shifts[half]:
            copy.wait_recv()
        for q in range(2):
            osel[half, q] = shift[half][steps[q]]
        occ_across.append(send(osel.at[half, 1 - xl], ofull.at[2, half], gsend, grecv, 14 + half, across))
        passed_occ.append(send(osel.at[half, 1 - xl], ofull.at[3, half], gsend, grecv, 16 + half, diagonal))
        occ_beside.append(send(osel.at[half, xl], ofull.at[1, half], gsend, grecv, 12 + half, sibling))
        ofull[0, half] = osel[half, xl]

    def project(number):
        slot, part = PIECES[number]
        for i in range(2):
            first = i * YZ
            e = efull[slot, part, :, first : first + YZ]
            first += part % 2 * QUART
            o = ofull[slot, part // 2, :, first : first + YZ]
            density = jnp.concatenate([o[v : v + 1] * e for v in range(NO)], axis=0)
            term = jnp.dot(density, yz[...], preferred_element_type=F32)
            first = (number * 2 + i) * 128
            ybuf[:, first : first + 128] = term.astype(BF16)

    def gathered(begin, end):
        return jnp.dot(ybuf[:, begin * 256 : end * 256], wtab[begin * 256 : end * 256, :], preferred_element_type=F32)

    lax.fori_loop(0, 16, fill, 0)
    select(0)
    cross(2)
    lax.fori_loop(16, 32, fill, 0)
    select(1)
    cross(3)
    for part in range(4):
        local[part].wait()
        project(part)
    occ_beside[0].wait_recv()
    occ_beside[1].wait_recv()
    for part in range(4):
        beside[part].wait_recv()
        project(4 + part)
    proj[...] = gathered(0, 8)
    ordering[...] = jnp.where(
        lax.broadcasted_iota(jnp.int32, (COLS, COLS), 0) == order_ref[...], 1.0, 0.0
    ).astype(BF16)

    oe = jnp.where(xl == 0, oe_shift[steps[0]], oe_shift[steps[1]])
    ee = jnp.broadcast_to(ee_ref[...].astype(F32), (NB, NE))
    spot = lax.broadcasted_iota(jnp.int32, (NB, NE), 1) - lax.broadcasted_iota(jnp.int32, (NB, NE), 0)
    weights = []
    for c in (core, 1 - core):
        level = jnp.sum(jnp.where(spot == c * NB, ee, 0.0), axis=1, keepdims=True)
        weights.append(jnp.concatenate([1.0 / (level - oe[v : v + 1, 0:1]) for v in range(NO)], axis=0))

    for part in range(4):
        if part % 2 == 0:
            occ_across[part // 2].wait_recv()
        theirs[part].wait_recv()
        project(8 + 2 * part)
        oblique[part].wait_recv()
        if part % 2 == 0:
            passed_occ[part // 2].wait_recv()
        project(9 + 2 * part)
        if part == 1:
            proj[...] = proj[...] + gathered(8, 12)
        if part == 2:
            proj[...] = proj[...] + gathered(12, 14)
    cols = pl.ds(pl.multiple_of(core * OWN, OWN), OWN)
    lefts[0] = ((proj[...] + gathered(14, 16)) * (1.0 / (4 * PTS))).astype(BF16)
    exchange = send(lefts.at[0], lefts.at[1], esend, erecv, 0, sibling)
    for who in range(2):
        if who:
            exchange.wait_recv()
        span = slice(who * PAIRS, who * PAIRS + PAIRS)
        right[span, :] = (weights[who] * lefts[who, :, cols].astype(F32)).astype(BF16)
        left_t[:, span] = lax.dot_general(
            ordering[...], lefts[who], (((1,), (1,)), ((), ())), preferred_element_type=F32
        ).astype(BF16)

    def a_block(y_):
        rows = pl.ds(pl.multiple_of(y_ * 96, 96), 96)
        return jnp.dot(left_t[rows, :], right[...], preferred_element_type=F32)

    def b_block(xh_):
        rows = pl.ds(pl.multiple_of(384 + xh_ * 192, 192), 192)
        return jnp.dot(left_t[rows, :], right[...], preferred_element_type=F32)

    gb[...] = b_block(1 - xh).astype(BF16)
    first_b = send(gb, rb, rsend, rrecv, 3, beyond)
    first_a, second_b = [], []
    for d in (2, 1, 3):
        ga[d - 1] = a_block((y + d) % 4).astype(BF16)
        first_a.append(send(ga.at[d - 1], ra.at[d - 1], rsend, rrecv, d - 1, y_peer[d - 1]))
    ta[...] = a_block(y)
    tb[...] = b_block(xh)

    for copy in first_a:
        copy.wait_recv()
    total = ta[...]
    for d in range(3):
        total = total + ra[d].astype(F32)
    ta[...] = total
    sa[...] = total.astype(BF16)
    rows = pl.ds(pl.multiple_of((1 - xh) * 48, 48), 48)
    second_a = send(sa.at[rows], qa, rsend, rrecv, 4, beyond)
    first_b.wait_recv()
    total = tb[...] + rb[...].astype(F32)
    tb[...] = total
    sb[...] = total.astype(BF16)
    for d in (2, 1, 3):
        rows = pl.ds(pl.multiple_of((y + d) % 4 * 48, 48), 48)
        second_b.append(send(sb.at[rows], qb.at[d - 1], rsend, rrecv, d + 4, y_peer[d - 1]))

    third = {}

    def ready(source, first):
        for to in range(4):
            rows = slice(to * 12, to * 12 + 16)
            tail = source[rows, 256:384].astype(BF16)
            for side in range(2):
                st[first + to, side, :, 0:128] = source[rows, side * 128 : side * 128 + 128].astype(BF16)
                st[first + to, side, :, 128:256] = tail

    second_a.wait_recv()
    fa[0:48, :] = ta[pl.ds(pl.multiple_of(xh * 48, 48), 48), :] + qa[...].astype(F32)
    ready(fa, 0)
    for copy in second_b:
        copy.wait_recv()
    total = tb[pl.ds(pl.multiple_of(y * 48, 48), 48), :]
    for d in range(3):
        total = total + qb[d].astype(F32)
    fb[0:48, :] = total
    ready(fb, 4)
    for d in (4, 3, 5, 2, 6, 1, 7, 0):
        for r in range(2):
            if d or r:
                side = xl if r == 0 else 1 - xl
                third[d, r] = send(st.at[(z + d) % 8, side], r3.at[d, r], fsend, frecv, d * 2 + r, z_peer[d][r])
    mine = st[z, xl].astype(F32)
    other = jnp.zeros((16, 256), F32)
    for d in (0, 1, 7, 2, 6, 3, 5, 4):
        if d:
            third[d, 0].wait_recv()
            mine = mine + r3[d, 0].astype(F32)
        third[d, 1].wait_recv()
        other = other + r3[d, 1].astype(F32)
    for q in range(2):
        total = jnp.where(xl == q, mine, other)[0:12]
        out_ref[q, :, 0:128] = total[:, 0:128]
        out_ref[q, :, 128:192] = jnp.where(xl == 0, total[:, 128:192], total[:, 192:256])
    for copy in sent:
        copy.wait_send()


def per_device(occupied, empty, occ_energy, emp_energy, partner, gvecs):
    waves = jnp.transpose(gvecs, (2, 0, 1))
    hbm = pl.BlockSpec(memory_space=pl.ANY)
    dma = pltpu.SemaphoreType.DMA
    return pl.pallas_call(
        kernel,
        out_shape=jax.ShapeDtypeStruct((2, 12, 192), F32),
        in_specs=[hbm] * 8,
        out_specs=pl.BlockSpec(memory_space=pltpu.VMEM),
        scratch_shapes=[
            pltpu.VMEM((1, NO), BF16),
            pltpu.VMEM((1, NE), BF16),
            pltpu.SMEM((2, 64), jnp.int32),
            pltpu.VMEM((3, 2, NG), jnp.int32),
            pltpu.VMEM((1, COLS), jnp.int32),
            pltpu.VMEM((3, NO, HALF), BF16),
            pltpu.VMEM((3, NO, HALF), BF16),
            pltpu.VMEM((NO, 128), F32),
            pltpu.VMEM((3, NO, 128), F32),
            pltpu.VMEM((4, 4, NB, QUART), BF16),
            pltpu.VMEM((2, 2, NO, HALF), BF16),
            pltpu.VMEM((4, 2, NO, HALF), BF16),
            pltpu.VMEM((YZ, 128), BF16),
            pltpu.VMEM((4096, COLS), BF16),
            pltpu.VMEM((32, COLS), F32),
            pltpu.VMEM((32, COLS), F32),
            pltpu.VMEM((PAIRS, 4096), BF16),
            pltpu.VMEM((PAIRS, COLS), F32),
            pltpu.VMEM((COLS, COLS), BF16),
            pltpu.VMEM((COLS, 2 * PAIRS), BF16),
            pltpu.VMEM((2 * PAIRS, OWN), BF16),
            pltpu.VMEM((2, PAIRS, COLS), BF16),
            pltpu.VMEM((3, 96, OWN), BF16),
            pltpu.VMEM((192, OWN), BF16),
            pltpu.VMEM((3, 96, OWN), BF16),
            pltpu.VMEM((192, OWN), BF16),
            pltpu.VMEM((96, OWN), F32),
            pltpu.VMEM((192, OWN), F32),
            pltpu.VMEM((96, OWN), BF16),
            pltpu.VMEM((192, OWN), BF16),
            pltpu.VMEM((48, OWN), BF16),
            pltpu.VMEM((3, 48, OWN), BF16),
            pltpu.VMEM((64, OWN), F32),
            pltpu.VMEM((64, OWN), F32),
            pltpu.VMEM((8, 2, 16, 256), BF16),
            pltpu.VMEM((8, 2, 16, 256), BF16),
            dma((9,)), dma((9,)), dma((18,)), dma((18,)), dma((8,)), dma((8,)), dma((16,)), dma((16,)), dma((1,)), dma((1,)), dma((10,)),
        ],
        compiler_params=pltpu.CompilerParams(
            collective_id=0, has_side_effects=True, vmem_limit_bytes=60 * 1024 * 1024
        ),
    )(
        occupied, empty, occ_energy, emp_energy, partner, waves,
        jnp.asarray(row_order()), jnp.asarray(yz_table()).astype(BF16),
    )


def solution(mesh):
    placed = (P("ka", None, "row"), P("ka", None, "row"), P("ka", None), P("ka", None), P(), P())
    return jax.shard_map(
        per_device, mesh=mesh, in_specs=placed, out_specs=P(None, "ka", "row"), check_vma=False
    )
```

```python
import math

import jax
import jax.numpy as jnp
import numpy as np
from jax import lax
from jax.experimental import pallas as pl
from jax.experimental.pallas import tpu as pltpu
from jax.sharding import PartitionSpec as P

MESH = pl.DeviceIdType.MESH
F32 = jnp.float32
BF16 = jnp.bfloat16
NO = 8
NE = 64
NB = 32
NG = 384
PTS = 4096
HALF = PTS // 2
QUART = PTS // 4
YZ = 512
GZ = 32
COLS = 2 * NG
OWN = COLS // 2
PAIRS = NO * NB
BLOCKS = (0, 1, 6, 7, 2, 8, 3, 4, 9, 10, 5, 11)
PIECES = tuple((slot, part) for slot in range(2) for part in range(4)) + tuple(
    (slot, part) for part in range(4) for slot in (2, 3)
)


def yz_table():
    point = np.arange(YZ)
    y, z = point // GZ, point % GZ
    table = np.zeros((YZ, 128), np.float64)
    for g1 in range(-4, 5):
        for g2 in range(5):
            turn = 2 * math.pi * ((g1 * y * 2 + g2 * z) % 32) / 32
            column = (g1 + 4) * 5 + g2
            table[:, column] = np.cos(turn)
            table[:, 64 + column] = np.sin(turn)
    return table.astype(np.float32)


def row_order():
    a = np.concatenate([np.arange(64) + 64 * block for block in BLOCKS])
    z, xh, y, i = a // 96, a // 48 % 2, a // 12 % 4, a % 12
    return (y * 192 + xh * 96 + z * 12 + i).astype(np.int32).reshape(1, COLS)


def kernel(
    occ_hbm, emp_hbm, oe_hbm, ee_hbm, partner_hbm, wave_hbm, order_hbm, yz_hbm, out_ref,
    oe_ref, ee_ref, partner_ref, wave_ref, order_ref,
    shift0, shift1, oe_src, oe_shift, efull, osel, ofull, yz, wtab, utab, vtab, ybuf, proj, ordering, left_t, right, lefts,
    ga, ra, fa, st, r3,
    zsend, zrecv, gsend, grecv, rsend, rrecv, fsend, frecv, esend, erecv, lsem,
):
    shift = (shift0, shift1)
    ka, row = lax.axis_index("ka"), lax.axis_index("row")
    z, xh, y = ka // 8, ka // 4 % 2, ka % 4
    xl, core = row // 2, row % 2

    def device(z_, xh_, y_, xl_, core_):
        return (z_ * 8 + xh_ * 4 + y_, xl_ * 2 + core_)

    sibling = device(z, xh, y, xl, 1 - core)
    diagonal = device(z, xh, y, 1 - xl, 1 - core)
    plane_peer = [device(z, (xh + n % 2) % 2, (y + n // 2) % 4, xl, core) for n in range(8)]
    z_peer = [[device((z + d) % 8, xh, y, xl if r == 0 else 1 - xl, core) for r in range(2)] for d in range(8)]
    across = z_peer[0][1]

    barrier = pltpu.get_barrier_semaphore()
    peers = [z_peer[d][r] for d in (4, 3, 5, 2, 6, 1, 7) for r in range(2)] + plane_peer[1:] + [diagonal, across, sibling]
    for peer in peers:
        pl.semaphore_signal(barrier, inc=1, device_id=peer, device_id_type=MESH)

    small = []
    for number, (src, dst) in enumerate(
        [(oe_hbm, oe_ref), (wave_hbm, wave_ref), (ee_hbm, ee_ref), (partner_hbm, partner_ref), (order_hbm, order_ref), (yz_hbm, yz)]
    ):
        small.append(pltpu.make_async_copy(src, dst, lsem.at[number]))
    local = []
    bands = [pl.ds(pl.multiple_of(c * NB, NB), NB) for c in (core, 1 - core)]
    points = [pl.ds(part * QUART, QUART) for part in range(4)]
    for part in range(4):
        local.append(pltpu.make_async_copy(emp_hbm.at[0, bands[0], points[part]], efull.at[0, part], lsem.at[6 + part]))
    for copy in small + local:
        copy.start()
    small[0].wait()

    eye = lax.broadcasted_iota(jnp.int32, (NO, NO), 0) == lax.broadcasted_iota(jnp.int32, (NO, NO), 1)
    levels = jnp.broadcast_to(oe_ref[...].astype(F32), (NO, NO))
    column = jnp.sum(jnp.where(eye, levels, 0.0), axis=1, keepdims=True)
    oe_src[...] = jnp.broadcast_to(column, (NO, 128))
    pl.semaphore_wait(barrier, len(peers))

    sent = []

    def send(src, dst, sends, recvs, index, peer):
        copy = pltpu.make_async_remote_copy(
            src_ref=src, dst_ref=dst, send_sem=sends.at[index], recv_sem=recvs.at[index],
            device_id=peer, device_id_type=MESH,
        )
        copy.start()
        sent.append(copy)
        return copy

    shifts, theirs, oblique, beside = [[], []], [], [], []

    def cross(part):
        theirs.append(send(emp_hbm.at[0, bands[0], points[part]], efull.at[2, part], gsend, grecv, part, across))
        oblique.append(send(emp_hbm.at[0, bands[1], points[part]], efull.at[3, part], gsend, grecv, 8 + part, diagonal))

    for half in range(2):
        for s in (2, 1, 3):
            src = occ_hbm.at[0, :, pl.ds(half * HALF, HALF)]
            shifts[half].append(send(src, shift[half].at[s - 1], zsend, zrecv, half * 3 + s - 1, z_peer[2 * s][0]))
    cross(0)
    cross(1)
    for s in range(1, 4):
        shifts[1].append(send(oe_src, oe_shift.at[s - 1], zsend, zrecv, 5 + s, z_peer[2 * s][0]))
    for part in range(4):
        beside.append(send(emp_hbm.at[0, bands[1], points[part]], efull.at[1, part], gsend, grecv, 4 + part, sibling))

    for copy in small[1:]:
        copy.wait()

    def kept(line):
        both = jnp.concatenate([line, line], axis=1)
        return jnp.concatenate([both[:, 64 * block : 64 * block + 64] for block in BLOCKS], axis=1)

    g0, g1, g2 = [
        kept(jnp.where(xl == 0, wave_ref[axis, 0:1, :], wave_ref[axis, 1:2, :])) for axis in range(3)
    ]
    flip = jnp.where(g2 < 0, -1, 1)
    group = (flip * g1 + 4) * 5 + flip * g2
    index = lax.broadcasted_iota(jnp.int32, (32, COLS), 0)
    late = index - 16
    slot_of = jnp.where(index < 16, index >> 3, 2 + ((late >> 1) & 1))
    plane_of = jnp.where(index < 16, index & 7, (late >> 2) * 2 + (late & 1))
    src_core = (core + slot_of) & 1
    src_xl = (xl + (slot_of >> 1)) & 1
    plane = (src_xl * 2 + src_core) * 8 + plane_of
    lane = lax.broadcasted_iota(jnp.int32, (32, COLS), 1)
    lane = jnp.where(lane < OWN, lane, lane - OWN)
    is_cos = (lane < 128) | ((lane >= 256) & (lane < 320))
    turn = ((g0 * plane - jnp.where(is_cos, 0, 8)) & 31).astype(F32) * (2.0 * math.pi / 32)
    utab[...] = jnp.cos(turn)
    vtab[...] = jnp.sin(turn) * (-flip).astype(F32)
    chosen = lax.broadcasted_iota(jnp.int32, (64, COLS), 0) == group

    def fill(i, carry):
        u = utab[pl.ds(i, 1), :]
        v = vtab[pl.ds(i, 1), :]
        base = pl.multiple_of(i * 128, 128)
        wtab[pl.ds(base, 64), :] = jnp.where(chosen, u, 0.0).astype(BF16)
        wtab[pl.ds(base + 64, 64), :] = jnp.where(chosen, v, 0.0).astype(BF16)
        return carry

    steps = [jnp.clip(partner_ref[q, 0] // 16, 1, 3) - 1 for q in range(2)]
    passed_occ, occ_beside, occ_across = [], [], []

    def select(half):
        for copy in shifts[half]:
            copy.wait_recv()
        for q in range(2):
            osel[half, q] = shift[half][steps[q]]
        occ_across.append(send(osel.at[half, 1 - xl], ofull.at[2, half], gsend, grecv, 14 + half, across))
        passed_occ.append(send(osel.at[half, 1 - xl], ofull.at[3, half], gsend, grecv, 16 + half, diagonal))
        occ_beside.append(send(osel.at[half, xl], ofull.at[1, half], gsend, grecv, 12 + half, sibling))
        ofull[0, half] = osel[half, xl]

    def project(number):
        slot, part = PIECES[number]
        for i in range(2):
            first = i * YZ
            e = efull[slot, part, :, first : first + YZ]
            first += part % 2 * QUART
            o = ofull[slot, part // 2, :, first : first + YZ]
            density = jnp.concatenate([o[v : v + 1] * e for v in range(NO)], axis=0)
            term = jnp.dot(density, yz[...], preferred_element_type=F32)
            first = (number * 2 + i) * 128
            ybuf[:, first : first + 128] = term.astype(BF16)

    def gathered(begin, end):
        return jnp.dot(ybuf[:, begin * 256 : end * 256], wtab[begin * 256 : end * 256, :], preferred_element_type=F32)

    lax.fori_loop(0, 16, fill, 0)
    select(0)
    cross(2)
    lax.fori_loop(16, 32, fill, 0)
    select(1)
    cross(3)
    for part in range(4):
        local[part].wait()
        project(part)
    occ_beside[0].wait_recv()
    occ_beside[1].wait_recv()
    for part in range(4):
        beside[part].wait_recv()
        project(4 + part)
    proj[...] = gathered(0, 8)
    ordering[...] = jnp.where(
        lax.broadcasted_iota(jnp.int32, (COLS, COLS), 0) == order_ref[...], 1.0, 0.0
    ).astype(BF16)

    oe = jnp.where(xl == 0, oe_shift[steps[0]], oe_shift[steps[1]])
    ee = jnp.broadcast_to(ee_ref[...].astype(F32), (NB, NE))
    spot = lax.broadcasted_iota(jnp.int32, (NB, NE), 1) - lax.broadcasted_iota(jnp.int32, (NB, NE), 0)
    weights = []
    for c in (core, 1 - core):
        level = jnp.sum(jnp.where(spot == c * NB, ee, 0.0), axis=1, keepdims=True)
        weights.append(jnp.concatenate([1.0 / (level - oe[v : v + 1, 0:1]) for v in range(NO)], axis=0))

    for part in range(4):
        if part % 2 == 0:
            occ_across[part // 2].wait_recv()
        theirs[part].wait_recv()
        project(8 + 2 * part)
        oblique[part].wait_recv()
        if part % 2 == 0:
            passed_occ[part // 2].wait_recv()
        project(9 + 2 * part)
        if part == 1:
            proj[...] = proj[...] + gathered(8, 12)
        if part == 2:
            proj[...] = proj[...] + gathered(12, 14)
    cols = pl.ds(pl.multiple_of(core * OWN, OWN), OWN)
    lefts[0] = ((proj[...] + gathered(14, 16)) * (1.0 / (4 * PTS))).astype(BF16)
    exchange = send(lefts.at[0], lefts.at[1], esend, erecv, 0, sibling)
    for who in range(2):
        if who:
            exchange.wait_recv()
        span = slice(who * PAIRS, who * PAIRS + PAIRS)
        right[span, :] = (weights[who] * lefts[who, :, cols].astype(F32)).astype(BF16)
        left_t[:, span] = lax.dot_general(
            ordering[...], lefts[who], (((1,), (1,)), ((), ())), preferred_element_type=F32
        ).astype(BF16)

    def block(n):
        rows = pl.ds(pl.multiple_of((y + n // 2) % 4 * 192 + (xh + n % 2) % 2 * 96, 96), 96)
        return jnp.dot(left_t[rows, :], right[...], preferred_element_type=F32)

    first = []
    for n in (5, 4, 3, 7, 1, 2, 6):
        ga[n - 1] = block(n).astype(BF16)
        first.append(send(ga.at[n - 1], ra.at[n - 1], rsend, rrecv, n - 1, plane_peer[n]))
    total = block(0)
    for copy in first:
        copy.wait_recv()
    for n in range(7):
        total = total + ra[n].astype(F32)
    fa[0:96, :] = total

    third = {}
    for to in range(8):
        rows = slice(to * 12, to * 12 + 16)
        tail = fa[rows, 256:384].astype(BF16)
        for side in range(2):
            st[to, side, :, 0:128] = fa[rows, side * 128 : side * 128 + 128].astype(BF16)
            st[to, side, :, 128:256] = tail
    for d in (4, 3, 5, 2, 6, 1, 7, 0):
        for r in range(2):
            if d or r:
                side = xl if r == 0 else 1 - xl
                third[d, r] = send(st.at[(z + d) % 8, side], r3.at[d, r], fsend, frecv, d * 2 + r, z_peer[d][r])
    mine = st[z, xl].astype(F32)
    other = jnp.zeros((16, 256), F32)
    for d in (0, 1, 7, 2, 6, 3, 5, 4):
        if d:
            third[d, 0].wait_recv()
            mine = mine + r3[d, 0].astype(F32)
        third[d, 1].wait_recv()
        other = other + r3[d, 1].astype(F32)
    for q in range(2):
        total = jnp.where(xl == q, mine, other)[0:12]
        out_ref[q, :, 0:128] = total[:, 0:128]
        out_ref[q, :, 128:192] = jnp.where(xl == 0, total[:, 128:192], total[:, 192:256])
    for copy in sent:
        copy.wait_send()


def per_device(occupied, empty, occ_energy, emp_energy, partner, gvecs):
    waves = jnp.transpose(gvecs, (2, 0, 1))
    hbm = pl.BlockSpec(memory_space=pl.ANY)
    dma = pltpu.SemaphoreType.DMA
    return pl.pallas_call(
        kernel,
        out_shape=jax.ShapeDtypeStruct((2, 12, 192), F32),
        in_specs=[hbm] * 8,
        out_specs=pl.BlockSpec(memory_space=pltpu.VMEM),
        scratch_shapes=[
            pltpu.VMEM((1, NO), BF16),
            pltpu.VMEM((1, NE), BF16),
            pltpu.SMEM((2, 64), jnp.int32),
            pltpu.VMEM((3, 2, NG), jnp.int32),
            pltpu.VMEM((1, COLS), jnp.int32),
            pltpu.VMEM((3, NO, HALF), BF16),
            pltpu.VMEM((3, NO, HALF), BF16),
            pltpu.VMEM((NO, 128), F32),
            pltpu.VMEM((3, NO, 128), F32),
            pltpu.VMEM((4, 4, NB, QUART), BF16),
            pltpu.VMEM((2, 2, NO, HALF), BF16),
            pltpu.VMEM((4, 2, NO, HALF), BF16),
            pltpu.VMEM((YZ, 128), BF16),
            pltpu.VMEM((4096, COLS), BF16),
            pltpu.VMEM((32, COLS), F32),
            pltpu.VMEM((32, COLS), F32),
            pltpu.VMEM((PAIRS, 4096), BF16),
            pltpu.VMEM((PAIRS, COLS), F32),
            pltpu.VMEM((COLS, COLS), BF16),
            pltpu.VMEM((COLS, 2 * PAIRS), BF16),
            pltpu.VMEM((2 * PAIRS, OWN), BF16),
            pltpu.VMEM((2, PAIRS, COLS), BF16),
            pltpu.VMEM((7, 96, OWN), BF16),
            pltpu.VMEM((7, 96, OWN), BF16),
            pltpu.VMEM((112, OWN), F32),
            pltpu.VMEM((8, 2, 16, 256), BF16),
            pltpu.VMEM((8, 2, 16, 256), BF16),
            dma((9,)), dma((9,)), dma((18,)), dma((18,)), dma((8,)), dma((8,)), dma((16,)), dma((16,)), dma((1,)), dma((1,)), dma((10,)),
        ],
        compiler_params=pltpu.CompilerParams(
            collective_id=0, has_side_effects=True, vmem_limit_bytes=60 * 1024 * 1024
        ),
    )(
        occupied, empty, occ_energy, emp_energy, partner, waves,
        jnp.asarray(row_order()), jnp.asarray(yz_table()).astype(BF16),
    )


def solution(mesh):
    placed = (P("ka", None, "row"), P("ka", None, "row"), P("ka", None), P("ka", None), P(), P())
    return jax.shard_map(
        per_device, mesh=mesh, in_specs=placed, out_specs=P(None, "ka", "row"), check_vma=False
    )
```

```python
import math

import jax
import jax.numpy as jnp
import numpy as np
from jax import lax
from jax.experimental import pallas as pl
from jax.experimental.pallas import tpu as pltpu
from jax.sharding import PartitionSpec as P

MESH = pl.DeviceIdType.MESH
F32 = jnp.float32
BF16 = jnp.bfloat16
NO = 8
NE = 64
NB = 32
NG = 384
PTS = 4096
HALF = PTS // 2
QUART = PTS // 4
YZ = 512
GZ = 32
COLS = 2 * NG
OWN = COLS // 2
PAIRS = NO * NB
BLOCKS = (0, 1, 6, 7, 2, 8, 3, 4, 9, 10, 5, 11)
PIECES = tuple((slot, part) for slot in range(2) for part in range(4)) + tuple(
    (slot, part) for part in range(4) for slot in (2, 3)
)


def yz_table():
    point = np.arange(YZ)
    y, z = point // GZ, point % GZ
    table = np.zeros((YZ, 128), np.float64)
    for g1 in range(-4, 5):
        for g2 in range(5):
            turn = 2 * math.pi * ((g1 * y * 2 + g2 * z) % 32) / 32
            column = (g1 + 4) * 5 + g2
            table[:, column] = np.cos(turn)
            table[:, 64 + column] = np.sin(turn)
    return table.astype(np.float32)


def row_order():
    a = np.concatenate([np.arange(64) + 64 * block for block in BLOCKS])
    z, xh, y, i = a // 96, a // 48 % 2, a // 12 % 4, a % 12
    return (y * 192 + xh * 96 + z * 12 + i).astype(np.int32).reshape(1, COLS)


def kernel(
    occ_hbm, emp_hbm, oe_hbm, ee_hbm, partner_hbm, wave_hbm, order_hbm, yz_hbm, out_ref,
    oe_ref, ee_ref, partner_ref, wave_ref, order_ref,
    shift0, shift1, oe_src, oe_shift, efull, osel, ofull, yz, wtab, utab, vtab, ybuf, proj, ordering, left_t, right, lefts,
    ga, ra, fa, st, r3,
    zsend, zrecv, gsend, grecv, rsend, rrecv, fsend, frecv, esend, erecv, lsem,
):
    shift = (shift0, shift1)
    ka, row = lax.axis_index("ka"), lax.axis_index("row")
    z, xh, y = ka // 8, ka // 4 % 2, ka % 4
    xl, core = row // 2, row % 2

    def device(z_, xh_, y_, xl_, core_):
        return (z_ * 8 + xh_ * 4 + y_, xl_ * 2 + core_)

    sibling = device(z, xh, y, xl, 1 - core)
    diagonal = device(z, xh, y, 1 - xl, 1 - core)
    plane_peer = [device(z, (xh + n % 2) % 2, (y + n // 2) % 4, xl, core) for n in range(8)]
    z_peer = [[device((z + d) % 8, xh, y, xl if r == 0 else 1 - xl, core) for r in range(2)] for d in range(8)]
    across = z_peer[0][1]

    barrier = pltpu.get_barrier_semaphore()
    peers = [z_peer[d][r] for d in (4, 3, 5, 2, 6, 1, 7) for r in range(2)] + plane_peer[1:] + [diagonal, across, sibling]
    for peer in peers:
        pl.semaphore_signal(barrier, inc=1, device_id=peer, device_id_type=MESH)

    small = []
    for number, (src, dst) in enumerate(
        [(oe_hbm, oe_ref), (wave_hbm, wave_ref), (ee_hbm, ee_ref), (partner_hbm, partner_ref), (order_hbm, order_ref), (yz_hbm, yz)]
    ):
        small.append(pltpu.make_async_copy(src, dst, lsem.at[number]))
    local = []
    bands = [pl.ds(pl.multiple_of(c * NB, NB), NB) for c in (core, 1 - core)]
    points = [pl.ds(part * QUART, QUART) for part in range(4)]
    for part in range(4):
        local.append(pltpu.make_async_copy(emp_hbm.at[0, bands[0], points[part]], efull.at[0, part], lsem.at[6 + part]))
    for copy in small + local:
        copy.start()
    small[0].wait()

    eye = lax.broadcasted_iota(jnp.int32, (NO, NO), 0) == lax.broadcasted_iota(jnp.int32, (NO, NO), 1)
    levels = jnp.broadcast_to(oe_ref[...].astype(F32), (NO, NO))
    column = jnp.sum(jnp.where(eye, levels, 0.0), axis=1, keepdims=True)
    oe_src[...] = jnp.broadcast_to(column, (NO, 128))
    pl.semaphore_wait(barrier, len(peers))

    sent = []

    def send(src, dst, sends, recvs, index, peer):
        copy = pltpu.make_async_remote_copy(
            src_ref=src, dst_ref=dst, send_sem=sends.at[index], recv_sem=recvs.at[index],
            device_id=peer, device_id_type=MESH,
        )
        copy.start()
        sent.append(copy)
        return copy

    shifts, theirs, oblique, beside = [[], []], [], [], []

    def cross(part):
        theirs.append(send(emp_hbm.at[0, bands[0], points[part]], efull.at[2, part], gsend, grecv, part, across))
        oblique.append(send(emp_hbm.at[0, bands[1], points[part]], efull.at[3, part], gsend, grecv, 8 + part, diagonal))

    for half in range(2):
        for s in (2, 1, 3):
            src = occ_hbm.at[0, :, pl.ds(half * HALF, HALF)]
            shifts[half].append(send(src, shift[half].at[s - 1], zsend, zrecv, half * 3 + s - 1, z_peer[2 * s][0]))
    cross(0)
    cross(1)
    for s in range(1, 4):
        shifts[1].append(send(oe_src, oe_shift.at[s - 1], zsend, zrecv, 5 + s, z_peer[2 * s][0]))
    for part in range(4):
        beside.append(send(emp_hbm.at[0, bands[1], points[part]], efull.at[1, part], gsend, grecv, 4 + part, sibling))

    for copy in small[1:]:
        copy.wait()

    def kept(line):
        both = jnp.concatenate([line, line], axis=1)
        return jnp.concatenate([both[:, 64 * block : 64 * block + 64] for block in BLOCKS], axis=1)

    g0, g1, g2 = [
        kept(jnp.where(xl == 0, wave_ref[axis, 0:1, :], wave_ref[axis, 1:2, :])) for axis in range(3)
    ]
    flip = jnp.where(g2 < 0, -1, 1)
    group = (flip * g1 + 4) * 5 + flip * g2
    index = lax.broadcasted_iota(jnp.int32, (32, COLS), 0)
    late = index - 16
    slot_of = jnp.where(index < 16, index >> 3, 2 + ((late >> 1) & 1))
    plane_of = jnp.where(index < 16, index & 7, (late >> 2) * 2 + (late & 1))
    src_core = (core + slot_of) & 1
    src_xl = (xl + (slot_of >> 1)) & 1
    plane = (src_xl * 2 + src_core) * 8 + plane_of
    lane = lax.broadcasted_iota(jnp.int32, (32, COLS), 1)
    lane = jnp.where(lane < OWN, lane, lane - OWN)
    is_cos = (lane < 128) | ((lane >= 256) & (lane < 320))
    turn = ((g0 * plane - jnp.where(is_cos, 0, 8)) & 31).astype(F32) * (2.0 * math.pi / 32)
    utab[...] = jnp.cos(turn)
    vtab[...] = jnp.sin(turn) * (-flip).astype(F32)
    chosen = lax.broadcasted_iota(jnp.int32, (64, COLS), 0) == group

    def fill(i, carry):
        u = utab[pl.ds(i, 1), :]
        v = vtab[pl.ds(i, 1), :]
        base = pl.multiple_of(i * 128, 128)
        wtab[pl.ds(base, 64), :] = jnp.where(chosen, u, 0.0).astype(BF16)
        wtab[pl.ds(base + 64, 64), :] = jnp.where(chosen, v, 0.0).astype(BF16)
        return carry

    steps = [jnp.clip(partner_ref[q, 0] // 16, 1, 3) - 1 for q in range(2)]
    passed_occ, occ_beside, occ_across = [], [], []

    def select(half):
        for copy in shifts[half]:
            copy.wait_recv()
        for q in range(2):
            osel[half, q] = shift[half][steps[q]]
        occ_across.append(send(osel.at[half, 1 - xl], ofull.at[2, half], gsend, grecv, 14 + half, across))
        passed_occ.append(send(osel.at[half, 1 - xl], ofull.at[3, half], gsend, grecv, 16 + half, diagonal))
        occ_beside.append(send(osel.at[half, xl], ofull.at[1, half], gsend, grecv, 12 + half, sibling))
        ofull[0, half] = osel[half, xl]

    def project(number):
        slot, part = PIECES[number]
        for i in range(2):
            first = i * YZ
            e = efull[slot, part, :, first : first + YZ]
            first += part % 2 * QUART
            o = ofull[slot, part // 2, :, first : first + YZ]
            density = jnp.concatenate([o[v : v + 1] * e for v in range(NO)], axis=0)
            term = jnp.dot(density, yz[...], preferred_element_type=F32)
            first = (number * 2 + i) * 128
            ybuf[:, first : first + 128] = term.astype(BF16)

    def gathered(begin, end):
        return jnp.dot(ybuf[:, begin * 256 : end * 256], wtab[begin * 256 : end * 256, :], preferred_element_type=F32)

    lax.fori_loop(0, 16, fill, 0)
    select(0)
    cross(2)
    lax.fori_loop(16, 32, fill, 0)
    select(1)
    cross(3)
    for part in range(4):
        local[part].wait()
        project(part)
    occ_beside[0].wait_recv()
    occ_beside[1].wait_recv()
    for part in range(4):
        beside[part].wait_recv()
        project(4 + part)
    proj[...] = gathered(0, 8)
    ordering[...] = jnp.where(
        lax.broadcasted_iota(jnp.int32, (COLS, COLS), 0) == order_ref[...], 1.0, 0.0
    ).astype(BF16)

    oe = jnp.where(xl == 0, oe_shift[steps[0]], oe_shift[steps[1]])
    ee = jnp.broadcast_to(ee_ref[...].astype(F32), (NB, NE))
    spot = lax.broadcasted_iota(jnp.int32, (NB, NE), 1) - lax.broadcasted_iota(jnp.int32, (NB, NE), 0)
    weights = []
    for c in (core, 1 - core):
        level = jnp.sum(jnp.where(spot == c * NB, ee, 0.0), axis=1, keepdims=True)
        weights.append(jnp.concatenate([1.0 / (level - oe[v : v + 1, 0:1]) for v in range(NO)], axis=0))

    for part in range(4):
        if part % 2 == 0:
            occ_across[part // 2].wait_recv()
        theirs[part].wait_recv()
        project(8 + 2 * part)
        oblique[part].wait_recv()
        if part % 2 == 0:
            passed_occ[part // 2].wait_recv()
        project(9 + 2 * part)
        if part == 1:
            proj[...] = proj[...] + gathered(8, 12)
        if part == 2:
            proj[...] = proj[...] + gathered(12, 14)
    cols = pl.ds(pl.multiple_of(core * OWN, OWN), OWN)
    lefts[0] = ((proj[...] + gathered(14, 16)) * (1.0 / (4 * PTS))).astype(BF16)
    exchange = send(lefts.at[0], lefts.at[1], esend, erecv, 0, sibling)
    for who in range(2):
        if who:
            exchange.wait_recv()
        span = slice(who * PAIRS, who * PAIRS + PAIRS)
        right[span, :] = (weights[who] * lefts[who, :, cols].astype(F32)).astype(BF16)
        left_t[:, span] = lax.dot_general(
            ordering[...], lefts[who], (((1,), (1,)), ((), ())), preferred_element_type=F32
        ).astype(BF16)

    def block(n):
        rows = pl.ds(pl.multiple_of((y + n // 2) % 4 * 192 + (xh + n % 2) % 2 * 96, 96), 96)
        return jnp.dot(left_t[rows, :], right[...], preferred_element_type=F32)

    first = []
    for n in (5, 3, 7, 4, 1, 2, 6):
        ga[n - 1] = block(n).astype(BF16)
        first.append(send(ga.at[n - 1], ra.at[n - 1], rsend, rrecv, n - 1, plane_peer[n]))
    total = block(0)
    for copy in first:
        copy.wait_recv()
    for n in range(7):
        total = total + ra[n].astype(F32)
    fa[0:96, :] = total

    third = {}
    for to in range(8):
        rows = slice(to * 12, to * 12 + 16)
        tail = fa[rows, 256:384].astype(BF16)
        for side in range(2):
            st[to, side, :, 0:128] = fa[rows, side * 128 : side * 128 + 128].astype(BF16)
            st[to, side, :, 128:256] = tail
    for d in (4, 3, 5, 2, 6, 1, 7, 0):
        for r in range(2):
            if d or r:
                side = xl if r == 0 else 1 - xl
                third[d, r] = send(st.at[(z + d) % 8, side], r3.at[d, r], fsend, frecv, d * 2 + r, z_peer[d][r])
    mine = st[z, xl].astype(F32)
    other = jnp.zeros((16, 256), F32)
    for d in (0, 1, 7, 2, 6, 3, 5, 4):
        if d:
            third[d, 0].wait_recv()
            mine = mine + r3[d, 0].astype(F32)
        third[d, 1].wait_recv()
        other = other + r3[d, 1].astype(F32)
    for q in range(2):
        total = jnp.where(xl == q, mine, other)[0:12]
        out_ref[q, :, 0:128] = total[:, 0:128]
        out_ref[q, :, 128:192] = jnp.where(xl == 0, total[:, 128:192], total[:, 192:256])
    for copy in sent:
        copy.wait_send()


def per_device(occupied, empty, occ_energy, emp_energy, partner, gvecs):
    waves = jnp.transpose(gvecs, (2, 0, 1))
    hbm = pl.BlockSpec(memory_space=pl.ANY)
    dma = pltpu.SemaphoreType.DMA
    return pl.pallas_call(
        kernel,
        out_shape=jax.ShapeDtypeStruct((2, 12, 192), F32),
        in_specs=[hbm] * 8,
        out_specs=pl.BlockSpec(memory_space=pltpu.VMEM),
        scratch_shapes=[
            pltpu.VMEM((1, NO), BF16),
            pltpu.VMEM((1, NE), BF16),
            pltpu.SMEM((2, 64), jnp.int32),
            pltpu.VMEM((3, 2, NG), jnp.int32),
            pltpu.VMEM((1, COLS), jnp.int32),
            pltpu.VMEM((3, NO, HALF), BF16),
            pltpu.VMEM((3, NO, HALF), BF16),
            pltpu.VMEM((NO, 128), F32),
            pltpu.VMEM((3, NO, 128), F32),
            pltpu.VMEM((4, 4, NB, QUART), BF16),
            pltpu.VMEM((2, 2, NO, HALF), BF16),
            pltpu.VMEM((4, 2, NO, HALF), BF16),
            pltpu.VMEM((YZ, 128), BF16),
            pltpu.VMEM((4096, COLS), BF16),
            pltpu.VMEM((32, COLS), F32),
            pltpu.VMEM((32, COLS), F32),
            pltpu.VMEM((PAIRS, 4096), BF16),
            pltpu.VMEM((PAIRS, COLS), F32),
            pltpu.VMEM((COLS, COLS), BF16),
            pltpu.VMEM((COLS, 2 * PAIRS), BF16),
            pltpu.VMEM((2 * PAIRS, OWN), BF16),
            pltpu.VMEM((2, PAIRS, COLS), BF16),
            pltpu.VMEM((7, 96, OWN), BF16),
            pltpu.VMEM((7, 96, OWN), BF16),
            pltpu.VMEM((112, OWN), F32),
            pltpu.VMEM((8, 2, 16, 256), BF16),
            pltpu.VMEM((8, 2, 16, 256), BF16),
            dma((9,)), dma((9,)), dma((18,)), dma((18,)), dma((8,)), dma((8,)), dma((16,)), dma((16,)), dma((1,)), dma((1,)), dma((10,)),
        ],
        compiler_params=pltpu.CompilerParams(
            collective_id=0, has_side_effects=True, vmem_limit_bytes=60 * 1024 * 1024
        ),
    )(
        occupied, empty, occ_energy, emp_energy, partner, waves,
        jnp.asarray(row_order()), jnp.asarray(yz_table()).astype(BF16),
    )


def solution(mesh):
    placed = (P("ka", None, "row"), P("ka", None, "row"), P("ka", None), P("ka", None), P(), P())
    return jax.shard_map(
        per_device, mesh=mesh, in_specs=placed, out_specs=P(None, "ka", "row"), check_vma=False
    )
```
